512 devices in a mesh: gx: 8 (over x, core), gy: 8 (over y), gz: 8 (over z).
Axes of the slice: x: 4, y: 8, z: 8, core: 2. Of those that a mesh axis runs over, the one named last changes fastest.
Arguments:
- loads: float32 [3, 64, 64, 1024], P(None, 'gx', 'gy', 'gz'), may hold values from -6 to 6
- density: float32 [64, 64, 1024], P('gx', 'gy', 'gz'), may hold values from 0.2 to 1
Outputs:
- solution: float32 [3, 64, 64, 1024], P(None, 'gx', 'gy', 'gz')
The draws below stay inside these ranges and needn't reach their ends.
All inputs are finite; a program needn't handle non-finite values.
Results may differ from the reference program's by a relative error of at most 0.0001.
Values sent between devices are 32-bit elements; how exact they have to be, the bound alone decides.
A program may use at most 64 MiB of HBM per device.

```python
import jax
import jax.numpy as jnp
from jax import lax

CASES = 3
LEVELS = 4
SWEEPS = 2
COARSE = 8
NX = 64
NY = 64
NZ = 1024


def block_levels(key, shape, cuts, smallest, largest):
    factor_of = 1.0
    for dim, parts in cuts:
        heights = jax.random.uniform(jax.random.fold_in(jax.random.fold_in(key, 6), dim), (parts,), jnp.float32, smallest / len(cuts), largest / len(cuts))
        factor_of = factor_of * jnp.repeat(jnp.exp(heights), shape[dim] // parts).reshape((-1,) + (1,) * (len(shape) - 1 - dim))
    return factor_of


def centred(key, extent, width, reach, split=(), held_as=jnp.bfloat16):
    gain = block_levels(key, extent, split, -0.22, 0.18) if split else 1.0
    drawn = jax.random.normal(key, extent, jnp.float32) * width * gain
    return jnp.minimum(jnp.maximum(drawn, -reach), reach).astype(held_as)


def setup_inputs(seed: int = 0) -> dict:
    streams_of = jax.random.split(jax.random.key(seed), 3)
    loads = centred(streams_of[0], (CASES, NX, NY, NZ), 1.0, 6.0, ((1, 8), (2, 8), (3, 8)), jnp.float32)
    density = jnp.clip(0.2 + 0.8 * jax.random.uniform(streams_of[1], (NX, NY, NZ), jnp.float32) ** block_levels(streams_of[1], (NX, NY, NZ), ((0, 8), (1, 8), (2, 8)), -0.2, 0.2), 0.2, 1.0)
    return dict(loads=loads, density=density)


damping = 0.6
floor_modulus = 0.001
offsets = [(bit_x, bit_y, bit_z) for bit_x in (0, 1) for bit_y in (0, 1) for bit_z in (0, 1)]


def differs_once(first, second):
    return sum(1 for place in range(3) if first[place] != second[place]) == 1


def take_block(array, start, count):
    return array[:, start[0]:start[0] + count[0], start[1]:start[1] + count[1], start[2]:start[2] + count[2]]


def apply_stiffness(padded_field, padded_moduli, scale):
    dims = padded_field.shape[1:]
    count = tuple(size - 1 for size in dims)
    out_count = tuple(size - 2 for size in dims)
    corner_values = {}
    for bits in offsets:
        corner_values[bits] = take_block(padded_field, bits, count)
    total = corner_values[offsets[0]]
    for bits in offsets[1:]:
        total = total + corner_values[bits]
    element = take_block(padded_moduli, (0, 0, 0), count)
    result = None
    for bits in offsets:
        edges = None
        for other in offsets:
            if differs_once(bits, other):
                edges = corner_values[other] if edges is None else edges + corner_values[other]
        contribution = element * (5.0 * corner_values[bits] + edges - total)
        start = (1 - bits[0], 1 - bits[1], 1 - bits[2])
        piece = take_block(contribution, start, out_count)
        result = piece if result is None else result + piece
    return result * (scale / 12.0)


def diagonal_of(padded_moduli, scale):
    out_count = tuple(size - 2 for size in padded_moduli.shape[1:])
    result = None
    for bits in offsets:
        piece = take_block(padded_moduli, (1 - bits[0], 1 - bits[1], 1 - bits[2]), out_count)
        result = piece if result is None else result + piece
    return result * (scale / 3.0)


def coarsen(moduli):
    shape = moduli.shape
    grouped = moduli.reshape(shape[0], shape[1] // 2, 2, shape[2] // 2, 2, shape[3] // 2, 2)
    return jnp.sum(grouped, axis=(2, 4, 6)) * 0.125


def restrict(padded):
    result = padded
    for axis in (1, 2, 3):
        core = result.shape[axis] - 2
        lower = lax.slice_in_dim(result, 0, core, 2, axis)
        middle = lax.slice_in_dim(result, 1, core + 1, 2, axis)
        upper = lax.slice_in_dim(result, 2, core + 2, 2, axis)
        result = middle + 0.5 * (lower + upper)
    return result


def prolong(padded):
    result = padded
    for axis in (1, 2, 3):
        core = result.shape[axis] - 2
        inner = lax.slice_in_dim(result, 1, core + 1, 1, axis)
        upper = lax.slice_in_dim(result, 2, core + 2, 1, axis)
        odd_nodes = 0.5 * (inner + upper)
        shape = list(inner.shape)
        shape[axis] = 2 * core
        result = jnp.stack([inner, odd_nodes], axis=axis + 1).reshape(shape)
    return result


def pad_one(array):
    return jnp.pad(array, ((0, 0), (1, 1), (1, 1), (1, 1)))


def vcycle(source, moduli_list):
    saved = []
    for section_no in range(LEVELS - 1):
        scale = 2.0 ** section_no
        moduli_near = pad_one(moduli_list[section_no])
        diag_now = diagonal_of(moduli_near, scale)
        current = damping * source / diag_now
        for repeat in range(SWEEPS - 1):
            current = current + damping * (source - apply_stiffness(pad_one(current), moduli_near, scale)) / diag_now
        residual = source - apply_stiffness(pad_one(current), moduli_near, scale)
        saved.append((current, source, moduli_near, diag_now))
        source = restrict(pad_one(residual))
    scale = 2.0 ** (LEVELS - 1)
    moduli_near = pad_one(moduli_list[LEVELS - 1])
    diag_now = diagonal_of(moduli_near, scale)
    current = damping * source / diag_now
    for repeat in range(COARSE - 1):
        current = current + damping * (source - apply_stiffness(pad_one(current), moduli_near, scale)) / diag_now
    for section_no in reversed(range(LEVELS - 1)):
        scale = 2.0 ** section_no
        kept, source, moduli_near, diag_now = saved[section_no]
        current = kept + prolong(pad_one(current))
        for repeat in range(SWEEPS):
            current = current + damping * (source - apply_stiffness(pad_one(current), moduli_near, scale)) / diag_now
    return current


def reference(loads, density):
    moduli = (floor_modulus + (1.0 - floor_modulus) * (density * density * density))[None]
    moduli_list = [moduli]
    for section_no in range(LEVELS - 1):
        moduli_list.append(coarsen(moduli_list[-1]))
    return lax.map(lambda single: vcycle(single[None], moduli_list)[0], loads)
```

```python
import functools
import itertools

import jax
import jax.numpy as jnp
from jax import lax
from jax.experimental import pallas as pl
from jax.experimental.pallas import tpu as pltpu
from jax.sharding import PartitionSpec as P

MESH = pl.DeviceIdType.MESH
F32 = jnp.float32
TILE = (8, 128)
SIDE = 8
ZHALO = 12
RING = (1, 2, 3, 4, -3, -2, -1)
XY8 = [(dx, dy) for dx in (-1, 0, 1) for dy in (-1, 0, 1) if dx or dy]
YZ23 = [(dy, dz) for dy in (0,) + RING for dz in (-1, 0, 1) if dy or dz]


def device(dx, dy, dz):
    return tuple(
        lax.rem(lax.axis_index(axis) + (step + SIDE), SIDE)
        for axis, step in (("gx", dx), ("gy", dy), ("gz", dz))
    )


def lanes():
    return lax.broadcasted_iota(jnp.int32, TILE, 1)


def rows():
    return lax.broadcasted_iota(jnp.int32, TILE, 0)


def up_plain(tile):
    return pltpu.roll(tile, 127, 1)


def down_plain(tile):
    return pltpu.roll(tile, 1, 1)


def up_pair(tile):
    turned = pltpu.roll(tile, 127, 1)
    return jnp.where(lanes() == 127, pltpu.roll(turned, 4, 0), turned)


def down_pair(tile):
    turned = pltpu.roll(tile, 1, 1)
    return jnp.where(lanes() == 0, pltpu.roll(turned, 4, 0), turned)


def twice(tile):
    return jnp.concatenate([tile, tile], axis=0)


def stencil(v, vp, m, ix, ys, mx, my, down):
    def column(y):
        held = {}
        for sx in (-1, 0, 1):
            a, b = v[ix + sx, y], vp[ix + sx, y]
            held[sx] = (a, b, a + b if sx else None)
        return held

    before, here = column(ys[0] - 1), column(ys[0])
    m_before = [m[mx - 1, ys[0] + my - 1], m[mx, ys[0] + my - 1]]
    for y in ys:
        after = column(y + 1)
        m_here = [m[mx - 1, y + my], m[mx, y + my]]
        above, below = None, None
        for sy, side, element in ((-1, before, m_before), (1, after, m_here)):
            for sx in (-1, 1):
                weight = element[0] if sx < 0 else element[1]
                both = side[sx][2]
                hi = weight * (both + (here[sx][1] + side[0][1]))
                lo = weight * (both + (here[sx][0] + side[0][0]))
                above = hi if above is None else above + hi
                below = lo if below is None else below + lo
        yield y, above + down(below)
        before, here, m_before = here, after, m_here


def loop(lower, upper, body):
    def step(i, carry):
        body(i)
        return carry

    lax.fori_loop(lower, upper, step, 0)


def diagonal(m, d4, inv, g, v, vp, xs, ys, up, down):
    def body(x):
        for y in ys:
            four = (m[x - 1, y - 1] + m[x - 1, y]) + (m[x, y - 1] + m[x, y])
            total = four + down(four)
            share = jnp.where(m[x, y] > 0.0, 0.15 / total, 0.0)
            d4[x, y] = 4.0 * total
            inv[x, y] = share
            first = share * g[x, y]
            v[x, y] = first
            vp[x, y] = up(first)

    loop(xs[0], xs[1], body)


def smooth(v, vp, m, inv, g, out, outp, xs, ys, up, down):
    def body(x):
        for y, around in stencil(v, vp, m, x, ys, x, 0, down):
            new = 0.4 * v[x, y] + inv[x, y] * (g[x, y] + around)
            out[x, y] = new
            outp[x, y] = up(new)

    loop(xs[0], xs[1], body)


def residual(v, vp, m, d4, g, out, xs, ys, down):
    def body(x):
        for y, around in stencil(v, vp, m, x, ys, x, 0, down):
            out[x, y] = (g[x, y] - d4[x, y] * v[x, y]) + around

    loop(xs[0], xs[1], body)


def restrict_xy(res, out, base, count):
    def body(i):
        x = base + 2 * i
        line = [
            res[x, y] + 0.5 * (res[x - 1, y] + res[x + 1, y])
            for y in range(base - 1, base + 2 * count)
        ]
        for k in range(count):
            out[i, k] = line[2 * k + 1] + 0.5 * (line[2 * k] + line[2 * k + 2])

    loop(0, count, body)


def coarsen_xy(m, out, base, count):
    def body(i):
        x = base + 2 * i
        for k in range(count):
            y = base + 2 * k
            out[i, k] = (m[x, y] + m[x, y + 1]) + (m[x + 1, y] + m[x + 1, y + 1])

    loop(0, count, body)


def place(index, own):
    if own == "all":
        return index
    if own == "beyond":
        return jnp.where(index < 64, index + 128, index - 128)
    return jnp.where(index < 96, index, index - 128)


def restriction(fine):
    f = place(lax.broadcasted_iota(jnp.int32, (128, 128), 0), fine)
    c = place(lax.broadcasted_iota(jnp.int32, (128, 128), 1), "round")
    gap = f - 2 * c
    return jnp.where(gap == 0, 0.5, jnp.where((gap == 1) | (gap == -1), 0.25, 0.0)).astype(F32)


def coarsening(fine):
    f = place(lax.broadcasted_iota(jnp.int32, (128, 128), 0), fine)
    c = place(lax.broadcasted_iota(jnp.int32, (128, 128), 1), "round")
    gap = f - 2 * c
    return jnp.where((gap == 0) | (gap == 1), 0.125, 0.0).astype(F32)


def prolongation(fine):
    c = place(lax.broadcasted_iota(jnp.int32, (128, 128), 0), "round")
    f = place(lax.broadcasted_iota(jnp.int32, (128, 128), 1), fine)
    gap = f - 2 * c
    return jnp.where(gap == 0, 1.0, jnp.where((gap == 1) | (gap == -1), 0.5, 0.0)).astype(F32)


def product(a, b):
    return jnp.dot(a, b, precision=lax.Precision.HIGHEST, preferred_element_type=F32)


def rise(source, mats, before, m, inv, g, zs, c, cp, a, ap, out, up, down):
    flat = source.reshape(7 * 7 * 8, 128)
    spread = product(flat, mats[0])
    if len(mats) == 2:
        top = lax.broadcasted_iota(jnp.int32, (7 * 7 * 8, 128), 0) % 8 < 4
        spread = jnp.where(top, spread, product(flat, mats[1]))
    zs[...] = spread.reshape(7, 7, 8, 128)
    m_ref, mx, my = m
    i_ref, ix, iy = inv
    g_ref, gx, gy = g

    def correct(i):
        for half in (0, 1):
            x = 2 * i + half
            line = [zs[i, k] if half == 0 else 0.5 * (zs[i, k] + zs[i + 1, k]) for k in range(7)]
            for y in range(12):
                k = y // 2
                add = line[k] if y % 2 == 0 else 0.5 * (line[k] + line[k + 1])
                new = jnp.where(m_ref[x + mx, y + my] > 0.0, before(x, y) + add, 0.0)
                c[x, y] = new
                cp[x, y] = up(new)

    loop(0, 6, correct)

    def sweep_a(x):
        for y, around in stencil(c, cp, m_ref, x, range(1, 11), x + mx, my, down):
            new = 0.4 * c[x, y] + i_ref[x + ix, y + iy] * (g_ref[x + gx, y + gy] + around)
            new = jnp.where(m_ref[x + mx, y + my] > 0.0, new, 0.0)
            a[x, y] = new
            ap[x, y] = up(new)

    loop(1, 11, sweep_a)

    def sweep_b(x):
        for y, around in stencil(a, ap, m_ref, x, range(2, 10), x + mx, my, down):
            new = 0.4 * a[x, y] + i_ref[x + ix, y + iy] * (g_ref[x + gx, y + gy] + around)
            new = jnp.where(m_ref[x + mx, y + my] > 0.0, new, 0.0)
            out(x - 2, y - 2, new)

    loop(2, 10, sweep_b)


def kernel(
    block, out, e0, zsend, zrecv, g0, m0, d0, i0, v0, vp0, u0, up0, r0,
    t1, tm1, e1, u1x, g1, m1, d1, i1, v1, vp1, u1, up1, r1,
    t2, tm2, yz, x2, g2, m2, d2, i2, v2, vp2, u2, up2, r2,
    t3, tm3, g3, m3, d3, i3, v3, vp3, u3, up3,
    zs, c, cp, a, ap, f2, f1,
    s0, q0, s1, q1, s1u, q1u, sy, qy, sx, qx,
):
    gx, gy, gz = (lax.axis_index(axis) for axis in ("gx", "gy", "gz"))

    partners = {(dx, dy, dz) for dx in (-1, 0, 1) for dy in (-1, 0, 1) for dz in (-1, 0, 1)}
    partners |= {(0, dy, dz) for dy, dz in YZ23} | {(dx, 0, 0) for dx in RING}
    partners = sorted(partners - {(0, 0, 0)})
    barrier = pltpu.get_barrier_semaphore()
    for o in partners:
        pl.semaphore_signal(barrier, inc=1, device_id=device(*o), device_id_type=MESH)

    for x in range(8):
        for y in range(0, 8, 2):
            pair = block[pl.ds((x * 8 + y) * 4, 8), :]
            e0[x + 4, y + 4] = pair[0:4]
            e0[x + 4, y + 5] = pair[4:8]
    k16 = lax.broadcasted_iota(jnp.int32, (16, 128), 0)
    l16 = lax.broadcasted_iota(jnp.int32, (16, 128), 1)
    pick_low = jnp.where((l16 == 128 - ZHALO + k16) & (k16 < ZHALO), 1.0, 0.0).astype(F32)
    pick_high = jnp.where((l16 == k16) & (k16 < ZHALO), 1.0, 0.0).astype(F32)
    for side, pick in enumerate((pick_low, pick_high)):
        for half in (0, 1):
            zsend[side, half] = lax.dot_general(
                pick, block[pl.ds(half * 128, 128), :], (((1,), (1,)), ((), ())),
                precision=lax.Precision.HIGHEST, preferred_element_type=F32,
            )

    zero = jnp.zeros(TILE, F32)

    def rim2(x):
        for y in range(28):
            m2[x, y] = zero

    loop(0, 28, rim2)
    for ref in (v2, vp2, u2, up2, r2):
        for i in range(5, 23):
            for j in (5, 22):
                ref[i, j] = zero
                ref[j, i] = zero

    def rim3(x):
        for y in range(16):
            for ref in (m3, v3, vp3, u3, up3):
                ref[x, y] = zero

    loop(0, 16, rim3)
    pl.semaphore_wait(barrier, len(partners))

    span = {-1: (4, 12, 3), 0: (4, 4, 8), 1: (8, 0, 4)}
    copies = []
    for n, (dx, dy) in enumerate(XY8):
        (ax, bx, cx), (ay, by, cy) = span[dx], span[dy]
        copies.append(
            pltpu.make_async_remote_copy(
                src_ref=e0.at[pl.ds(ax, cx), pl.ds(ay, cy)],
                dst_ref=e0.at[pl.ds(bx, cx), pl.ds(by, cy)],
                send_sem=s0.at[n], recv_sem=q0.at[n],
                device_id=device(dx, dy, 0), device_id_type=MESH,
            )
        )
    n = 8
    for dz in (-1, 1):
        side = 0 if dz > 0 else 1
        for dx, dy in itertools.product((-1, 0, 1), repeat=2):
            first, count = {-1: (0, 1), 0: (0, 2), 1: (1, 1)}[dx]
            copies.append(
                pltpu.make_async_remote_copy(
                    src_ref=zsend.at[side, pl.ds(first, count)],
                    dst_ref=zrecv.at[side, 1 - dx, 1 - dy, pl.ds(first, count)],
                    send_sem=s0.at[n], recv_sem=q0.at[n],
                    device_id=device(dx, dy, dz), device_id_type=MESH,
                )
            )
            n += 1
    for copy in copies:
        copy.start()
    for copy in copies:
        copy.wait()

    top = rows() < 4
    lane = lanes()
    beyond_ok = ((lane < ZHALO) & (gz < SIDE - 1)) | ((lane >= 128 - ZHALO) & (gz > 0))
    known = top | beyond_ok
    put = jnp.concatenate([pick_low, pick_high], axis=0)
    for rx, ry in itertools.product((-1, 0, 1), repeat=2):
        x_from, x_to = {-1: (-4, 0), 0: (0, 8), 1: (8, 11)}[rx]
        y_from, y_to = {-1: (-4, 0), 0: (0, 8), 1: (8, 11)}[ry]
        inside = None
        if rx:
            inside = gx > 0 if rx < 0 else gx < SIDE - 1
        if ry:
            more = gy > 0 if ry < 0 else gy < SIDE - 1
            inside = more if inside is None else inside & more
        ok = known if inside is None else known & inside
        for half in {-1: (1,), 0: (0, 1), 1: (0,)}[rx]:
            both = jnp.concatenate([zrecv[0, rx + 1, ry + 1, half], zrecv[1, rx + 1, ry + 1, half]], axis=0)
            ends = lax.dot_general(
                both, put, (((0,), (0,)), ((), ())),
                precision=lax.Precision.HIGHEST, preferred_element_type=F32,
            )
            for x in range(x_from, x_to):
                source_x = x % 8
                if source_x // 4 != half:
                    continue
                for y in range(y_from, y_to):
                    at = ((source_x % 4) * 8 + y % 8) * 4
                    held = ends[at // 8 * 8 : at // 8 * 8 + 8]
                    if at % 8 == 0:
                        held = pltpu.roll(held, 4, 0)
                    own = e0[x + 4, y + 4]
                    whole = jnp.where(top, twice(own), held)
                    dens = jnp.where(top, jnp.broadcast_to(whole[3:4], TILE), jnp.broadcast_to(whole[7:8], TILE))
                    g0[x + 4, y + 4] = jnp.where(ok, 1.8 * whole, 0.0)
                    m0[x + 4, y + 4] = jnp.where(
                        ok, 0.15 * (0.001 + (1.0 - 0.001) * (dens * dens * dens)), 0.0
                    )

    diagonal(m0, d0, i0, g0, v0, vp0, (1, 15), range(1, 15), up_pair, down_pair)
    smooth(v0, vp0, m0, i0, g0, u0, up0, (2, 14), range(2, 14), up_pair, down_pair)
    residual(u0, up0, m0, d0, g0, r0, (3, 12), range(3, 12), down_pair)
    restrict_xy(r0, t1, 4, 4)
    coarsen_xy(m0, tm1, 4, 4)
    top128 = lax.broadcasted_iota(jnp.int32, (128, 128), 0) % 8 < 4
    flat = t1[...].reshape(128, 128)
    new_g = jnp.where(top128, product(flat, restriction("all")), product(flat, restriction("beyond")))
    flat = tm1[...].reshape(128, 128)
    new_m = jnp.where(top128, product(flat, coarsening("all")), product(flat, coarsening("beyond")))
    for x in range(4):
        for y in range(4):
            at = (x * 4 + y) * 8
            tg = new_g[at : at + 8]
            tm = new_m[at : at + 8]
            tg = tg + pltpu.roll(tg, 4, 0)
            tm = tm + pltpu.roll(tm, 4, 0)
            e1[x + 4, y + 4] = jnp.where(rows() == 3, tm, tg)[0:4]

    def blocks8(ref, send, recv):
        found = []
        for n, (dx, dy) in enumerate(XY8):
            found.append(
                pltpu.make_async_remote_copy(
                    src_ref=ref.at[pl.ds(4, 4), pl.ds(4, 4)],
                    dst_ref=ref.at[pl.ds({-1: 8, 0: 4, 1: 0}[dx], 4), pl.ds({-1: 8, 0: 4, 1: 0}[dy], 4)],
                    send_sem=send.at[n], recv_sem=recv.at[n],
                    device_id=device(dx, dy, 0), device_id_type=MESH,
                )
            )
        return found

    copies = blocks8(e1, s1, q1)
    for copy in copies:
        copy.start()
    for copy in copies:
        copy.wait()

    def take1(x):
        inside_x = jnp.where(((x >= 4) | (gx > 0)) & ((x < 8) | (gx < SIDE - 1)), 1.0, 0.0)
        for y in range(12):
            factor = inside_x
            if y < 4:
                factor = factor * jnp.where(gy > 0, 1.0, 0.0)
            if y >= 8:
                factor = factor * jnp.where(gy < SIDE - 1, 1.0, 0.0)
            whole = twice(e1[x, y]) * factor
            mod = jnp.broadcast_to(whole[3:4], TILE)
            m1[x, y] = mod
            g1[x, y] = jnp.where(mod > 0.0, whole, 0.0)

    loop(0, 12, take1)
    diagonal(m1, d1, i1, g1, v1, vp1, (1, 12), range(1, 12), up_plain, down_plain)
    smooth(v1, vp1, m1, i1, g1, u1, up1, (2, 9), range(2, 9), up_plain, down_plain)
    for x in range(4):
        for y in range(4):
            u1x[x + 4, y + 4] = u1[x + 4, y + 4][0:4]
    u_copies = blocks8(u1x, s1u, q1u)
    residual(u1, up1, m1, d1, g1, r1, (3, 8), range(3, 8), down_plain)
    restrict_xy(r1, t2, 4, 2)
    coarsen_xy(m1, tm2, 4, 2)
    new_g = product(t2[...].reshape(32, 128), restriction("round"))
    new_m = product(tm2[...].reshape(32, 128), coarsening("round"))
    for x in range(2):
        for y in range(2):
            at = (x * 2 + y) * 8
            both = jnp.where(rows() == 3, new_m[at : at + 8], new_g[at : at + 8])
            both = jnp.where(lane < 32, both, 0.0)
            yz[1, x, 2 * gy + y] = both[0:4]

    copies = []
    for n, (dy, dz) in enumerate(YZ23):
        copies.append(
            pltpu.make_async_remote_copy(
                src_ref=yz.at[1, :, pl.ds(2 * gy, 2)],
                dst_ref=yz.at[1 - dz, :, pl.ds(2 * gy, 2)],
                send_sem=sy.at[n], recv_sem=qy.at[n],
                device_id=device(0, dy, dz), device_id_type=MESH,
            )
        )
    for copy in copies:
        copy.start()
    for copy in u_copies:
        copy.start()
    for copy in copies:
        copy.wait()
    low_ok = jnp.where(gz > 0, 1.0, 0.0)
    high_ok = jnp.where(gz < SIDE - 1, 1.0, 0.0)
    for x in range(2):
        for y in range(16):
            x2[2 * gx + x, y] = (
                yz[1, x, y]
                + pltpu.roll(yz[0, x, y], 96, 1) * low_ok
                + pltpu.roll(yz[2, x, y], 32, 1) * high_ok
            )

    copies = []
    for n, dx in enumerate(RING):
        copies.append(
            pltpu.make_async_remote_copy(
                src_ref=x2.at[pl.ds(2 * gx, 2)],
                dst_ref=x2.at[pl.ds(2 * gx, 2)],
                send_sem=sx.at[n], recv_sem=qx.at[n],
                device_id=device(dx, 0, 0), device_id_type=MESH,
            )
        )
    for copy in copies:
        copy.start()
    for copy in copies:
        copy.wait()

    def take2(x):
        for y in range(16):
            whole = twice(x2[x, y])
            mod = jnp.broadcast_to(whole[3:4], TILE)
            m2[x + 6, y + 6] = mod
            g2[x + 6, y + 6] = jnp.where(mod > 0.0, whole, 0.0)

    loop(0, 16, take2)
    diagonal(m2, d2, i2, g2, v2, vp2, (6, 22), range(6, 22), up_plain, down_plain)
    smooth(v2, vp2, m2, i2, g2, u2, up2, (6, 22), range(6, 22), up_plain, down_plain)
    residual(u2, up2, m2, d2, g2, r2, (6, 22), range(6, 22), down_plain)
    restrict_xy(r2, t3, 6, 8)
    coarsen_xy(m2, tm3, 6, 8)
    new_g = product(t3[...].reshape(512, 128), restriction("round")).reshape(8, 8, 8, 128)
    new_m = product(tm3[...].reshape(512, 128), coarsening("round")).reshape(8, 8, 8, 128)
    m3[pl.ds(4, 8), pl.ds(4, 8)] = new_m
    g3[pl.ds(4, 8), pl.ds(4, 8)] = jnp.where(new_m > 0.0, new_g, 0.0)

    diagonal(m3, d3, i3, g3, v3, vp3, (4, 12), range(4, 12), up_plain, down_plain)

    def two(i):
        smooth(v3, vp3, m3, i3, g3, u3, up3, (4, 12), range(4, 12), up_plain, down_plain)
        smooth(u3, up3, m3, i3, g3, v3, vp3, (4, 12), range(4, 12), up_plain, down_plain)

    loop(0, 3, two)
    smooth(v3, vp3, m3, i3, g3, u3, up3, (4, 12), range(4, 12), up_plain, down_plain)

    def keep(ref):
        def store(x, y, new):
            ref[x, y] = new

        return store

    x_at, y_at = 2 * gx + 2, 2 * gy + 2
    rise(
        u3[pl.ds(gx + 2, 7), pl.ds(gy + 2, 7)],
        (prolongation("round"),),
        lambda x, y: u2[x + x_at, y + y_at],
        (m2, x_at, y_at), (i2, x_at, y_at), (g2, x_at, y_at),
        zs, c, cp, a, ap, keep(f2), up_plain, down_plain,
    )
    for copy in u_copies:
        copy.wait()
    rise(
        f2[pl.ds(0, 7), pl.ds(0, 7)],
        (prolongation("round"),),
        lambda x, y: twice(u1x[x, y]),
        (m1, 0, 0), (i1, 0, 0), (g1, 0, 0),
        zs, c, cp, a, ap, keep(f1), up_plain, down_plain,
    )

    def finish(x, y, new):
        out[pl.ds(pl.multiple_of((x * 8 + y) * 8, 8), 8), :] = new

    rise(
        f1[pl.ds(1, 7), pl.ds(1, 7)],
        (prolongation("all"), prolongation("beyond")),
        lambda x, y: u0[x + 2, y + 2],
        (m0, 2, 2), (i0, 2, 2), (g0, 2, 2),
        zs, c, cp, a, ap, finish, up_pair, down_pair,
    )


def per_device(loads, density):
    block = jnp.concatenate([jnp.transpose(loads, (1, 2, 0, 3)), density[:, :, None]], axis=2)

    def tiles(*lead):
        return pltpu.VMEM(lead + TILE, F32)

    def thin(*lead):
        return pltpu.VMEM(lead + (4, 128), F32)

    sems = []
    for count in (26, 8, 8, 23, 7):
        sems += [pltpu.SemaphoreType.DMA((count,))] * 2
    result = pl.pallas_call(
        kernel,
        out_shape=jax.ShapeDtypeStruct((512, 128), F32),
        in_specs=[pl.BlockSpec(memory_space=pltpu.VMEM)],
        out_specs=pl.BlockSpec(memory_space=pltpu.VMEM),
        scratch_shapes=[thin(15, 15), pltpu.VMEM((2, 2, 16, 128), F32), pltpu.VMEM((2, 3, 3, 2, 16, 128), F32)]
        + [tiles(15, 15)] * 9
        + [tiles(4, 4)] * 2
        + [thin(12, 12)] * 2
        + [tiles(12, 12)] * 9
        + [tiles(2, 2)] * 2
        + [thin(3, 2, 16), thin(16, 16)]
        + [tiles(28, 28)] * 9
        + [tiles(8, 8)] * 2
        + [tiles(16, 16)] * 8
        + [tiles(7, 7)]
        + [tiles(12, 12)] * 4
        + [tiles(8, 8)] * 2
        + sems,
        compiler_params=pltpu.CompilerParams(
            collective_id=0, has_side_effects=True, vmem_limit_bytes=60 * 2**20
        ),
        cost_estimate=pl.CostEstimate(flops=10**8, bytes_accessed=10**6, transcendentals=0),
    )(block.reshape(256, 128))
    return jnp.transpose(result.reshape(8, 8, 8, 128)[:, :, :3], (2, 0, 1, 3))


def solution(mesh):
    placed = (P(None, "gx", "gy", "gz"), P("gx", "gy", "gz"))
    return jax.shard_map(
        per_device, mesh=mesh, in_specs=placed, out_specs=P(None, "gx", "gy", "gz"), check_vma=False
    )
```

```python
import functools
import itertools

import jax
import jax.numpy as jnp
from jax import lax
from jax.experimental import pallas as pl
from jax.experimental.pallas import tpu as pltpu
from jax.sharding import PartitionSpec as P

MESH = pl.DeviceIdType.MESH
F32 = jnp.float32
TILE = (8, 128)
SIDE = 8
UNROLL = 8
ZHALO = 12
RING = (1, 2, 3, 4, -3, -2, -1)
XY8 = [(dx, dy) for dx in (-1, 0, 1) for dy in (-1, 0, 1) if dx or dy]
YZ23 = [(dy, dz) for dy in (0,) + RING for dz in (-1, 0, 1) if dy or dz]


def device(dx, dy, dz):
    return tuple(
        lax.rem(lax.axis_index(axis) + (step + SIDE), SIDE)
        for axis, step in (("gx", dx), ("gy", dy), ("gz", dz))
    )


def lanes(shape=TILE):
    return lax.broadcasted_iota(jnp.int32, shape, len(shape) - 1)


def rows(shape=TILE):
    return lax.broadcasted_iota(jnp.int32, shape, len(shape) - 2)


def turn_rows(tiles, by):
    return pltpu.roll(tiles, by, tiles.ndim - 2)


def turn_lanes(tiles, by):
    return pltpu.roll(tiles, by, tiles.ndim - 1)


def up_plain(tiles):
    return turn_lanes(tiles, 127)


def down_plain(tiles):
    return turn_lanes(tiles, 1)


def up_pair(tiles):
    turned = turn_lanes(tiles, 127)
    return jnp.where(lanes(tiles.shape) == 127, turn_rows(turned, 4), turned)


def down_pair(tiles):
    turned = turn_lanes(tiles, 1)
    return jnp.where(lanes(tiles.shape) == 0, turn_rows(turned, 4), turned)


def twice(tiles):
    return jnp.concatenate([tiles, tiles], axis=tiles.ndim - 2)


def spread(tiles, row):
    return jnp.broadcast_to(tiles[..., row : row + 1, :], tiles.shape)


def stencil(v, vp, m, ix, y0, n, mx, my, down):
    wide = pl.ds(y0 - 1, n + 2)
    lower = {sx: v[ix + sx, wide] for sx in (-1, 0, 1)}
    upper = {sx: vp[ix + sx, wide] for sx in (-1, 0, 1)}
    weights = {-1: m[mx - 1, pl.ds(y0 + my - 1, n + 1)], 1: m[mx, pl.ds(y0 + my - 1, n + 1)]}
    above, below = None, None
    for sx in (-1, 1):
        both = lower[sx] + upper[sx]
        for sy in (-1, 1):
            side = slice(1 + sy, 1 + sy + n)
            weight = weights[sx][0:n] if sy < 0 else weights[sx][1 : n + 1]
            hi = weight * (both[side] + (upper[sx][1 : n + 1] + upper[0][side]))
            lo = weight * (both[side] + (lower[sx][1 : n + 1] + lower[0][side]))
            above = hi if above is None else above + hi
            below = lo if below is None else below + lo
    return above + down(below)


def loop(lower, upper, body):
    count = upper - lower
    each = max(k for k in range(1, UNROLL + 1) if count % k == 0)

    def step(i, carry):
        for k in range(each):
            body(lower + i * each + k)
        return carry

    if each == count:
        step(0, 0)
    else:
        lax.fori_loop(0, count // each, step, 0)


def diagonal(m, d4, inv, g, v, vp, xs, ys, up, down):
    y0, n = ys
    at = pl.ds(y0, n)

    def body(x):
        pairs = m[x - 1, pl.ds(y0 - 1, n + 1)] + m[x, pl.ds(y0 - 1, n + 1)]
        four = pairs[0:n] + pairs[1 : n + 1]
        total = four + down(four)
        share = jnp.where(m[x, at] > 0.0, 0.15 / total, 0.0)
        d4[x, at] = 4.0 * total
        inv[x, at] = share
        first = share * g[x, at]
        v[x, at] = first
        vp[x, at] = up(first)

    loop(xs[0], xs[1], body)


def smooth(v, vp, m, inv, g, out, outp, xs, ys, up, down):
    y0, n = ys
    at = pl.ds(y0, n)

    def body(x):
        around = stencil(v, vp, m, x, y0, n, x, 0, down)
        new = 0.4 * v[x, at] + inv[x, at] * (g[x, at] + around)
        out[x, at] = new
        outp[x, at] = up(new)

    loop(xs[0], xs[1], body)


def residual(v, vp, m, d4, g, out, xs, ys, down):
    y0, n = ys
    at = pl.ds(y0, n)

    def body(x):
        around = stencil(v, vp, m, x, y0, n, x, 0, down)
        out[x, at] = (g[x, at] - d4[x, at] * v[x, at]) + around

    loop(xs[0], xs[1], body)


def restrict_xy(res, out, base, count):
    def body(i):
        x = base + 2 * i
        wide = pl.ds(base - 1, 2 * count + 1)
        line = res[x, wide] + 0.5 * (res[x - 1, wide] + res[x + 1, wide])
        for k in range(count):
            out[i, k] = line[2 * k + 1] + 0.5 * (line[2 * k] + line[2 * k + 2])

    loop(0, count, body)


def coarsen_xy(m, out, base, count):
    def body(i):
        x = base + 2 * i
        wide = pl.ds(base, 2 * count)
        line = m[x, wide] + m[x + 1, wide]
        for k in range(count):
            out[i, k] = line[2 * k] + line[2 * k + 1]

    loop(0, count, body)


def place(index, own):
    if own == "all":
        return index
    if own == "beyond":
        return jnp.where(index < 64, index + 128, index - 128)
    return jnp.where(index < 96, index, index - 128)


def restriction(fine):
    f = place(lax.broadcasted_iota(jnp.int32, (128, 128), 0), fine)
    c = place(lax.broadcasted_iota(jnp.int32, (128, 128), 1), "round")
    gap = f - 2 * c
    return jnp.where(gap == 0, 0.5, jnp.where((gap == 1) | (gap == -1), 0.25, 0.0)).astype(F32)


def coarsening(fine):
    f = place(lax.broadcasted_iota(jnp.int32, (128, 128), 0), fine)
    c = place(lax.broadcasted_iota(jnp.int32, (128, 128), 1), "round")
    gap = f - 2 * c
    return jnp.where((gap == 0) | (gap == 1), 0.125, 0.0).astype(F32)


def prolongation(fine):
    c = place(lax.broadcasted_iota(jnp.int32, (128, 128), 0), "round")
    f = place(lax.broadcasted_iota(jnp.int32, (128, 128), 1), fine)
    gap = f - 2 * c
    return jnp.where(gap == 0, 1.0, jnp.where((gap == 1) | (gap == -1), 0.5, 0.0)).astype(F32)


def product(a, b):
    return jnp.dot(a, b, precision=lax.Precision.HIGHEST, preferred_element_type=F32)


def rise(source, mats, before, m, inv, g, zs, c, cp, a, ap, out, up, down):
    flat = source.reshape(7 * 7 * 8, 128)
    wide = product(flat, mats[0])
    if len(mats) == 2:
        top = lax.broadcasted_iota(jnp.int32, (7 * 7 * 8, 128), 0) % 8 < 4
        wide = jnp.where(top, wide, product(flat, mats[1]))
    zs[...] = wide.reshape(7, 7, 8, 128)
    m_ref, mx, my = m
    i_ref, ix, iy = inv
    g_ref, gx, gy = g

    def correct(i):
        for half in (0, 1):
            x = 2 * i + half
            line = zs[i] if half == 0 else 0.5 * (zs[i] + zs[i + 1])
            middle = 0.5 * (line[0:6] + line[1:7])
            add = jnp.stack([line[0:6], middle], axis=1).reshape((12,) + TILE)
            new = jnp.where(m_ref[x + mx, pl.ds(my, 12)] > 0.0, before(x) + add, 0.0)
            c[x] = new
            cp[x] = up(new)

    loop(0, 6, correct)

    def sweep(old, oldp, x, y0, n):
        around = stencil(old, oldp, m_ref, x, y0, n, x + mx, my, down)
        new = 0.4 * old[x, pl.ds(y0, n)] + i_ref[x + ix, pl.ds(y0 + iy, n)] * (
            g_ref[x + gx, pl.ds(y0 + gy, n)] + around
        )
        return jnp.where(m_ref[x + mx, pl.ds(y0 + my, n)] > 0.0, new, 0.0)

    def sweep_a(x):
        new = sweep(c, cp, x, 1, 10)
        a[x, pl.ds(1, 10)] = new
        ap[x, pl.ds(1, 10)] = up(new)

    loop(1, 11, sweep_a)

    def sweep_b(x):
        out[x - 2] = sweep(a, ap, x, 2, 8)

    loop(2, 10, sweep_b)


def kernel(
    loads, density, out, held_loads, held_density, block, e0, zsend, zrecv, g0, m0, d0, i0, v0, vp0, u0, up0, r0,
    t1, tm1, e1, u1x, g1, m1, d1, i1, v1, vp1, u1, up1, r1,
    t2, tm2, yz, x2, g2, m2, d2, i2, v2, vp2, u2, up2, r2,
    t3, tm3, g3, m3, d3, i3, v3, vp3, u3, up3,
    zs, c, cp, a, ap, f2, f1, f0,
    sin, s0, q0, s1, q1, s1u, q1u, sy, qy, sx, qx,
):
    gx, gy, gz = (lax.axis_index(axis) for axis in ("gx", "gy", "gz"))

    inputs = [
        pltpu.make_async_copy(loads, held_loads, sin.at[0]),
        pltpu.make_async_copy(density, held_density, sin.at[1]),
    ]
    for copy in inputs:
        copy.start()

    partners = {(dx, dy, dz) for dx in (-1, 0, 1) for dy in (-1, 0, 1) for dz in (-1, 0, 1)}
    partners |= {(0, dy, dz) for dy, dz in YZ23} | {(dx, 0, 0) for dx in RING}
    partners = sorted(partners - {(0, 0, 0)})
    barrier = pltpu.get_barrier_semaphore()
    for o in partners:
        pl.semaphore_signal(barrier, inc=1, device_id=device(*o), device_id_type=MESH)

    for copy in inputs:
        copy.wait()
    field = rows((8,) + TILE) % 4
    four = [held_loads[0], held_loads[1], held_loads[2], held_density[...]]
    for y in range(4):
        pair = turn_rows(four[3], (3 - y) % 8) if y != 3 else four[3]
        for f in range(3):
            pair = jnp.where(field == f, turn_rows(four[f], (f - y) % 8) if f != y else four[f], pair)
        block[:, y] = pair
        e0[pl.ds(4, 8), y + 4] = pair[:, 0:4]
        e0[pl.ds(4, 8), y + 8] = pair[:, 4:8]
    pl.semaphore_wait(barrier, len(partners))

    span = {-1: (4, 12, 3), 0: (4, 4, 8), 1: (8, 0, 4)}
    sent = []
    copies = []
    for n, (dx, dy) in enumerate(XY8):
        (ax, bx, cx), (ay, by, cy) = span[dx], span[dy]
        copies.append(
            pltpu.make_async_remote_copy(
                src_ref=e0.at[pl.ds(ax, cx), pl.ds(ay, cy)],
                dst_ref=e0.at[pl.ds(bx, cx), pl.ds(by, cy)],
                send_sem=s0.at[n], recv_sem=q0.at[n],
                device_id=device(dx, dy, 0), device_id_type=MESH,
            )
        )
        copies[-1].start()
    k16 = lax.broadcasted_iota(jnp.int32, (16, 128), 0)
    l16 = lax.broadcasted_iota(jnp.int32, (16, 128), 1)
    pick_low = jnp.where((l16 == 128 - ZHALO + k16) & (k16 < ZHALO), 1.0, 0.0).astype(F32)
    pick_high = jnp.where((l16 == k16) & (k16 < ZHALO), 1.0, 0.0).astype(F32)
    n = 8
    for dz, pick in ((-1, pick_high), (1, pick_low)):
        side = 0 if dz > 0 else 1
        for half in (0, 1):
            zsend[side, half] = lax.dot_general(
                pick, block[pl.ds(half * 4, 4)].reshape(128, 128), (((1,), (1,)), ((), ())),
                precision=lax.Precision.HIGHEST, preferred_element_type=F32,
            )
        for dx, dy in itertools.product((-1, 0, 1), repeat=2):
            first, count = {-1: (0, 1), 0: (0, 2), 1: (1, 1)}[dx]
            copies.append(
                pltpu.make_async_remote_copy(
                    src_ref=zsend.at[side, pl.ds(first, count)],
                    dst_ref=zrecv.at[side, 1 - dx, 1 - dy, pl.ds(first, count)],
                    send_sem=s0.at[n], recv_sem=q0.at[n],
                    device_id=device(dx, dy, dz), device_id_type=MESH,
                )
            )
            copies[-1].start()
            n += 1

    def rim2(x):
        m2[x] = jnp.zeros((28,) + TILE, F32)

    loop(0, 28, rim2)
    for ref in (v2, vp2, u2, up2, r2):
        for j in (5, 22):
            ref[j, pl.ds(5, 18)] = jnp.zeros((18,) + TILE, F32)
            ref[pl.ds(5, 18), j] = jnp.zeros((18,) + TILE, F32)

    def rim3(x):
        for ref in (m3, v3, vp3, u3, up3):
            ref[x] = jnp.zeros((16,) + TILE, F32)

    loop(0, 16, rim3)
    for copy in copies:
        copy.wait_recv()
    sent += copies

    low_in, high_in = jnp.where(gz > 0, 1.0, 0.0), jnp.where(gz < SIDE - 1, 1.0, 0.0)
    put = jnp.concatenate([pick_low, pick_high], axis=0)
    for rx, ry in itertools.product((-1, 0, 1), repeat=2):
        inside = None
        if rx:
            inside = gx > 0 if rx < 0 else gx < SIDE - 1
        if ry:
            more = gy > 0 if ry < 0 else gy < SIDE - 1
            inside = more if inside is None else inside & more
        factor = 1.0 if inside is None else jnp.where(inside, 1.0, 0.0)
        for half in {-1: (1,), 0: (0, 1), 1: (0,)}[rx]:
            both = jnp.concatenate([zrecv[0, rx + 1, ry + 1, half], zrecv[1, rx + 1, ry + 1, half]], axis=0)
            ends = lax.dot_general(
                both, put, (((0,), (0,)), ((), ())),
                precision=lax.Precision.HIGHEST, preferred_element_type=F32,
            ).reshape((4, 4) + TILE)
            x_at, nx = 4 + 8 * rx + 4 * half, 3 if rx > 0 else 4
            for late in {-1: (1,), 0: (0, 1), 1: (0,)}[ry]:
                y_at, ny = 4 + 8 * ry + 4 * late, 3 if ry > 0 else 4
                shape = (nx, ny) + TILE
                spot = (pl.ds(x_at, nx), pl.ds(y_at, ny))
                top, lane = rows(shape) < 4, lanes(shape)
                held = ends[0:nx, 0:ny]
                if not late:
                    held = turn_rows(held, 4)
                whole = jnp.where(top, twice(e0[spot]), held)
                dens = jnp.where(top, spread(whole, 3), spread(whole, 7))
                ok = jnp.where(
                    top, 1.0,
                    jnp.where(lane < ZHALO, high_in, jnp.where(lane >= 128 - ZHALO, low_in, 0.0)),
                ) * factor
                g0[spot] = (1.8 * ok) * whole
                m0[spot] = (0.15 * ok) * (0.001 + (1.0 - 0.001) * (dens * dens * dens))

    diagonal(m0, d0, i0, g0, v0, vp0, (1, 15), (1, 14), up_pair, down_pair)
    smooth(v0, vp0, m0, i0, g0, u0, up0, (2, 14), (2, 12), up_pair, down_pair)
    residual(u0, up0, m0, d0, g0, r0, (3, 12), (3, 9), down_pair)
    restrict_xy(r0, t1, 4, 4)
    coarsen_xy(m0, tm1, 4, 4)
    top128 = rows((16,) + TILE) < 4

    def both_ends(tiles, kind):
        flat = tiles[...].reshape(128, 128)
        parts = [product(flat, kind(where)).reshape((16,) + TILE) for where in ("all", "beyond")]
        joined = jnp.where(top128, parts[0], parts[1])
        return joined + turn_rows(joined, 4)

    new_g, new_m = both_ends(t1, restriction), both_ends(tm1, coarsening)
    joined = jnp.where(rows((16,) + TILE) == 3, new_m, new_g)[:, 0:4]
    e1[pl.ds(4, 4), pl.ds(4, 4)] = joined.reshape(4, 4, 4, 128)

    def blocks8(ref, send, recv):
        found = []
        for n, (dx, dy) in enumerate(XY8):
            found.append(
                pltpu.make_async_remote_copy(
                    src_ref=ref.at[pl.ds(4, 4), pl.ds(4, 4)],
                    dst_ref=ref.at[pl.ds({-1: 8, 0: 4, 1: 0}[dx], 4), pl.ds({-1: 8, 0: 4, 1: 0}[dy], 4)],
                    send_sem=send.at[n], recv_sem=recv.at[n],
                    device_id=device(dx, dy, 0), device_id_type=MESH,
                )
            )
        return found

    copies = blocks8(e1, s1, q1)
    for copy in copies:
        copy.start()
    for copy in copies:
        copy.wait_recv()
    sent += copies

    y_index = lax.broadcasted_iota(jnp.int32, (12,) + TILE, 0)
    inside_y = jnp.where(y_index < 4, jnp.where(gy > 0, 1.0, 0.0), jnp.where(y_index < 8, 1.0, jnp.where(gy < SIDE - 1, 1.0, 0.0)))

    def take1(x):
        inside_x = jnp.where(((x >= 4) | (gx > 0)) & ((x < 8) | (gx < SIDE - 1)), 1.0, 0.0)
        whole = twice(e1[x]) * (inside_x * inside_y)
        mod = spread(whole, 3)
        m1[x] = mod
        g1[x] = jnp.where(mod > 0.0, whole, 0.0)

    loop(0, 12, take1)
    diagonal(m1, d1, i1, g1, v1, vp1, (1, 12), (1, 11), up_plain, down_plain)
    smooth(v1, vp1, m1, i1, g1, u1, up1, (2, 9), (2, 7), up_plain, down_plain)
    own = (pl.ds(4, 4), pl.ds(4, 4))
    u1x[own] = u1[own][:, :, 0:4]
    u_copies = blocks8(u1x, s1u, q1u)
    residual(u1, up1, m1, d1, g1, r1, (3, 8), (3, 5), down_plain)
    restrict_xy(r1, t2, 4, 2)
    coarsen_xy(m1, tm2, 4, 2)
    new_g = product(t2[...].reshape(32, 128), restriction("round"))
    new_m = product(tm2[...].reshape(32, 128), coarsening("round"))
    both = jnp.where(rows((32, 128)) % 8 == 3, new_m, new_g)
    both = jnp.where(lanes((32, 128)) < 32, both, 0.0).reshape((2, 2) + TILE)
    yz[1, :, pl.ds(2 * gy, 2)] = both[:, :, 0:4]

    copies = []
    for n, (dy, dz) in enumerate(YZ23):
        copies.append(
            pltpu.make_async_remote_copy(
                src_ref=yz.at[1, :, pl.ds(2 * gy, 2)],
                dst_ref=yz.at[1 - dz, :, pl.ds(2 * gy, 2)],
                send_sem=sy.at[n], recv_sem=qy.at[n],
                device_id=device(0, dy, dz), device_id_type=MESH,
            )
        )
    for copy in copies + u_copies:
        copy.start()
    for copy in copies:
        copy.wait_recv()
    sent += copies + u_copies
    x2[pl.ds(2 * gx, 2)] = (
        yz[1] + turn_lanes(yz[0], 96) * low_in + turn_lanes(yz[2], 32) * high_in
    )

    copies = []
    for n, dx in enumerate(RING):
        copies.append(
            pltpu.make_async_remote_copy(
                src_ref=x2.at[pl.ds(2 * gx, 2)],
                dst_ref=x2.at[pl.ds(2 * gx, 2)],
                send_sem=sx.at[n], recv_sem=qx.at[n],
                device_id=device(dx, 0, 0), device_id_type=MESH,
            )
        )
    for copy in copies:
        copy.start()
    for copy in copies:
        copy.wait_recv()
    sent += copies

    def take2(x):
        whole = twice(x2[x])
        mod = spread(whole, 3)
        m2[x + 6, pl.ds(6, 16)] = mod
        g2[x + 6, pl.ds(6, 16)] = jnp.where(mod > 0.0, whole, 0.0)

    loop(0, 16, take2)
    diagonal(m2, d2, i2, g2, v2, vp2, (6, 22), (6, 16), up_plain, down_plain)
    smooth(v2, vp2, m2, i2, g2, u2, up2, (6, 22), (6, 16), up_plain, down_plain)
    residual(u2, up2, m2, d2, g2, r2, (6, 22), (6, 16), down_plain)
    restrict_xy(r2, t3, 6, 8)
    coarsen_xy(m2, tm3, 6, 8)
    new_g = product(t3[...].reshape(512, 128), restriction("round")).reshape(8, 8, 8, 128)
    new_m = product(tm3[...].reshape(512, 128), coarsening("round")).reshape(8, 8, 8, 128)
    m3[pl.ds(4, 8), pl.ds(4, 8)] = new_m
    g3[pl.ds(4, 8), pl.ds(4, 8)] = jnp.where(new_m > 0.0, new_g, 0.0)

    diagonal(m3, d3, i3, g3, v3, vp3, (4, 12), (4, 8), up_plain, down_plain)

    def two(i):
        smooth(v3, vp3, m3, i3, g3, u3, up3, (4, 12), (4, 8), up_plain, down_plain)
        smooth(u3, up3, m3, i3, g3, v3, vp3, (4, 12), (4, 8), up_plain, down_plain)

    loop(0, 3, two)
    smooth(v3, vp3, m3, i3, g3, u3, up3, (4, 12), (4, 8), up_plain, down_plain)

    x_at, y_at = 2 * gx + 2, 2 * gy + 2
    rise(
        u3[pl.ds(gx + 2, 7), pl.ds(gy + 2, 7)],
        (prolongation("round"),),
        lambda x: u2[x + x_at, pl.ds(y_at, 12)],
        (m2, x_at, y_at), (i2, x_at, y_at), (g2, x_at, y_at),
        zs, c, cp, a, ap, f2, up_plain, down_plain,
    )
    for copy in u_copies:
        copy.wait_recv()
    rise(
        f2[pl.ds(0, 7), pl.ds(0, 7)],
        (prolongation("round"),),
        lambda x: twice(u1x[x]),
        (m1, 0, 0), (i1, 0, 0), (g1, 0, 0),
        zs, c, cp, a, ap, f1, up_plain, down_plain,
    )

    rise(
        f1[pl.ds(1, 7), pl.ds(1, 7)],
        (prolongation("all"), prolongation("beyond")),
        lambda x: u0[x + 2, pl.ds(2, 12)],
        (m0, 2, 2), (i0, 2, 2), (g0, 2, 2),
        zs, c, cp, a, ap, f0, up_pair, down_pair,
    )
    for f in range(3):
        plane = f0[:, f]
        for y in range(8):
            if y != f:
                plane = jnp.where(rows((8,) + TILE) == y, turn_rows(f0[:, y], (y - f) % 8), plane)
        out[f] = plane
    for copy in sent:
        copy.wait_send()


def per_device(loads, density):
    def tiles(*lead):
        return pltpu.VMEM(lead + TILE, F32)

    def thin(*lead):
        return pltpu.VMEM(lead + (4, 128), F32)

    sems = [pltpu.SemaphoreType.DMA((2,))]
    for count in (26, 8, 8, 23, 7):
        sems += [pltpu.SemaphoreType.DMA((count,))] * 2
    return pl.pallas_call(
        kernel,
        out_shape=jax.ShapeDtypeStruct((3,) + (8,) + TILE, F32),
        in_specs=[pl.BlockSpec(memory_space=pl.ANY)] * 2,
        out_specs=pl.BlockSpec(memory_space=pltpu.VMEM),
        scratch_shapes=[tiles(3, 8), tiles(8), tiles(8, 4), thin(15, 15), pltpu.VMEM((2, 2, 16, 128), F32), pltpu.VMEM((2, 3, 3, 2, 16, 128), F32)]
        + [tiles(15, 15)] * 9
        + [tiles(4, 4)] * 2
        + [thin(12, 12)] * 2
        + [tiles(12, 12)] * 9
        + [tiles(2, 2)] * 2
        + [thin(3, 2, 16), thin(16, 16)]
        + [tiles(28, 28)] * 9
        + [tiles(8, 8)] * 2
        + [tiles(16, 16)] * 8
        + [tiles(7, 7)]
        + [tiles(12, 12)] * 4
        + [tiles(8, 8)] * 3
        + sems,
        compiler_params=pltpu.CompilerParams(
            collective_id=0, has_side_effects=True, vmem_limit_bytes=60 * 2**20
        ),
        cost_estimate=pl.CostEstimate(flops=10**8, bytes_accessed=10**6, transcendentals=0),
    )(loads, density)


def solution(mesh):
    placed = (P(None, "gx", "gy", "gz"), P("gx", "gy", "gz"))
    return jax.shard_map(
        per_device, mesh=mesh, in_specs=placed, out_specs=P(None, "gx", "gy", "gz"), check_vma=False
    )
```

```python
import functools
import itertools

import jax
import jax.numpy as jnp
from jax import lax
from jax.experimental import pallas as pl
from jax.experimental.pallas import tpu as pltpu
from jax.sharding import PartitionSpec as P

MESH = pl.DeviceIdType.MESH
F32 = jnp.float32
TILE = (8, 128)
SIDE = 8
UNROLL = 8
ZHALO = 12
RING = (1, 2, 3, 4, -3, -2, -1)
XY8 = [(dx, dy) for dx in (-1, 0, 1) for dy in (-1, 0, 1) if dx or dy]
YZ23 = [(dy, dz) for dy in (0,) + RING for dz in (-1, 0, 1) if dy or dz]


def device(dx, dy, dz):
    return tuple(
        lax.rem(lax.axis_index(axis) + (step + SIDE), SIDE)
        for axis, step in (("gx", dx), ("gy", dy), ("gz", dz))
    )


def lanes(shape=TILE):
    return lax.broadcasted_iota(jnp.int32, shape, len(shape) - 1)


def rows(shape=TILE):
    return lax.broadcasted_iota(jnp.int32, shape, len(shape) - 2)


def turn_rows(tiles, by):
    return pltpu.roll(tiles, by, tiles.ndim - 2)


def turn_lanes(tiles, by):
    return pltpu.roll(tiles, by, tiles.ndim - 1)


def up_plain(tiles):
    return turn_lanes(tiles, 127)


def down_plain(tiles):
    return turn_lanes(tiles, 1)


def up_pair(tiles):
    turned = turn_lanes(tiles, 127)
    return jnp.where(lanes(tiles.shape) == 127, turn_rows(turned, 4), turned)


def down_pair(tiles):
    turned = turn_lanes(tiles, 1)
    return jnp.where(lanes(tiles.shape) == 0, turn_rows(turned, 4), turned)


def twice(tiles):
    return jnp.concatenate([tiles, tiles], axis=tiles.ndim - 2)


def spread(tiles, row):
    return jnp.broadcast_to(tiles[..., row : row + 1, :], tiles.shape)


def halves(tiles):
    top, turned = rows(tiles.shape) < 4, turn_rows(tiles, 4)
    return jnp.where(top, tiles, turned), jnp.where(top, turned, tiles)


def put_rims(ref, x, line):
    top, n = rows() < 4, line.shape[0]
    ref[x, 0] = jnp.where(top, 0.0, turn_rows(line[n - 1], 4))
    ref[x, n + 1] = jnp.where(top, turn_rows(line[0], 4), 0.0)


def stencil(v, vp, m, ix, y0, n, mx, my, down):
    wide = pl.ds(y0 - 1, n + 2)
    lower = {sx: v[ix + sx, wide] for sx in (-1, 0, 1)}
    upper = {sx: vp[ix + sx, wide] for sx in (-1, 0, 1)}
    weights = {-1: m[mx - 1, pl.ds(y0 + my - 1, n + 1)], 1: m[mx, pl.ds(y0 + my - 1, n + 1)]}
    above, below = None, None
    for sx in (-1, 1):
        both = lower[sx] + upper[sx]
        for sy in (-1, 1):
            side = slice(1 + sy, 1 + sy + n)
            weight = weights[sx][0:n] if sy < 0 else weights[sx][1 : n + 1]
            hi = weight * (both[side] + (upper[sx][1 : n + 1] + upper[0][side]))
            lo = weight * (both[side] + (lower[sx][1 : n + 1] + lower[0][side]))
            above = hi if above is None else above + hi
            below = lo if below is None else below + lo
    return above + down(below)


def loop(lower, upper, body):
    count = upper - lower
    each = max(k for k in range(1, UNROLL + 1) if count % k == 0)

    def step(i, carry):
        for k in range(each):
            body(lower + i * each + k)
        return carry

    if each == count:
        step(0, 0)
    else:
        lax.fori_loop(0, count // each, step, 0)


def loop_rolled(lower, upper, body):
    def step(i, carry):
        body(i)
        return carry

    lax.fori_loop(lower, upper, step, 0)


def diagonal(m, d4, inv, g, v, vp, xs, ys, up, down, rims=False, also=None):
    y0, n = ys
    at = pl.ds(y0, n)

    def body(x):
        pairs = m[x - 1, pl.ds(y0 - 1, n + 1)] + m[x, pl.ds(y0 - 1, n + 1)]
        four = pairs[0:n] + pairs[1 : n + 1]
        total = four + down(four)
        share = jnp.where(m[x, at] > 0.0, 0.15 / total, 0.0)
        d4[x, at] = 4.0 * total
        inv[x, at] = share
        first = share * g[x, at]
        above = up(first)
        v[x, at] = first
        vp[x, at] = above
        if rims:
            put_rims(v, x, first)
            put_rims(vp, x, above)
        if also is not None:
            also(x, share)

    loop(xs[0], xs[1], body)


def smooth(v, vp, m, inv, g, out, outp, xs, ys, up, down, rims=False, also=None):
    y0, n = ys
    at = pl.ds(y0, n)

    def body(x):
        around = stencil(v, vp, m, x, y0, n, x, 0, down)
        new = 0.4 * v[x, at] + inv[x, at] * (g[x, at] + around)
        above = up(new)
        out[x, at] = new
        outp[x, at] = above
        if rims:
            put_rims(out, x, new)
            put_rims(outp, x, above)
        if also is not None:
            also(x, new)

    loop(xs[0], xs[1], body)


def residual(v, vp, m, d4, g, out, xs, ys, down, rims=False):
    y0, n = ys
    at = pl.ds(y0, n)

    def body(x):
        around = stencil(v, vp, m, x, y0, n, x, 0, down)
        left = (g[x, at] - d4[x, at] * v[x, at]) + around
        out[x, at] = left
        if rims:
            put_rims(out, x, left)

    loop(xs[0], xs[1], body)


def restrict_xy(res, out, base, count_x, count):
    def body(i):
        x = base + 2 * i
        wide = pl.ds(base - 1, 2 * count + 1)
        line = res[x, wide] + 0.5 * (res[x - 1, wide] + res[x + 1, wide])
        for k in range(count):
            out[i, k] = line[2 * k + 1] + 0.5 * (line[2 * k] + line[2 * k + 2])

    loop(0, count_x, body)


def coarsen_xy(m, out, base, count_x, count):
    def body(i):
        x = base + 2 * i
        wide = pl.ds(base, 2 * count)
        line = m[x, wide] + m[x + 1, wide]
        for k in range(count):
            out[i, k] = line[2 * k] + line[2 * k + 1]

    loop(0, count_x, body)


def place(index, own):
    if own == "all":
        return index
    if own == "beyond":
        return jnp.where(index < 64, index + 128, index - 128)
    return jnp.where(index < 96, index, index - 128)


def restriction(fine):
    f = place(lax.broadcasted_iota(jnp.int32, (128, 128), 0), fine)
    c = place(lax.broadcasted_iota(jnp.int32, (128, 128), 1), "round")
    gap = f - 2 * c
    return jnp.where(gap == 0, 0.5, jnp.where((gap == 1) | (gap == -1), 0.25, 0.0)).astype(F32)


def coarsening(fine):
    f = place(lax.broadcasted_iota(jnp.int32, (128, 128), 0), fine)
    c = place(lax.broadcasted_iota(jnp.int32, (128, 128), 1), "round")
    gap = f - 2 * c
    return jnp.where((gap == 0) | (gap == 1), 0.125, 0.0).astype(F32)


def prolongation(fine):
    c = place(lax.broadcasted_iota(jnp.int32, (128, 128), 0), "round")
    f = place(lax.broadcasted_iota(jnp.int32, (128, 128), 1), fine)
    gap = f - 2 * c
    return jnp.where(gap == 0, 1.0, jnp.where((gap == 1) | (gap == -1), 0.5, 0.0)).astype(F32)


def product(a, b):
    return jnp.dot(a, b, precision=lax.Precision.HIGHEST, preferred_element_type=F32)


def rise(source, mats, before, m, inv, g, zs, c, cp, a, ap, out, up, down):
    flat = source.reshape(7 * 7 * 8, 128)
    wide = product(flat, mats[0])
    if len(mats) == 2:
        top = lax.broadcasted_iota(jnp.int32, (7 * 7 * 8, 128), 0) % 8 < 4
        wide = jnp.where(top, wide, product(flat, mats[1]))
    zs[...] = wide.reshape(7, 7, 8, 128)
    m_ref, mx, my = m
    i_ref, ix, iy = inv
    g_ref, gx, gy = g

    def correct(i):
        for half in (0, 1):
            x = 2 * i + half
            line = zs[i] if half == 0 else 0.5 * (zs[i] + zs[i + 1])
            middle = 0.5 * (line[0:6] + line[1:7])
            add = jnp.stack([line[0:6], middle], axis=1).reshape((12,) + TILE)
            new = jnp.where(m_ref[x + mx, pl.ds(my, 12)] > 0.0, before(x) + add, 0.0)
            c[x] = new
            cp[x] = up(new)

    loop(0, 6, correct)

    def sweep(old, oldp, x, y0, n):
        around = stencil(old, oldp, m_ref, x, y0, n, x + mx, my, down)
        new = 0.4 * old[x, pl.ds(y0, n)] + i_ref[x + ix, pl.ds(y0 + iy, n)] * (
            g_ref[x + gx, pl.ds(y0 + gy, n)] + around
        )
        return jnp.where(m_ref[x + mx, pl.ds(y0 + my, n)] > 0.0, new, 0.0)

    def sweep_a(x):
        new = sweep(c, cp, x, 1, 10)
        a[x, pl.ds(1, 10)] = new
        ap[x, pl.ds(1, 10)] = up(new)

    loop(1, 11, sweep_a)

    def sweep_b(x):
        out[x - 2] = sweep(a, ap, x, 2, 8)

    loop(2, 10, sweep_b)


def kernel(
    loads, density, out, held_loads, held_density, block, e0, zsend, zrecv, g0, m0, d0, i0, v0, vp0, u0, up0, r0,
    t1, tm1, e1, u1x, g1, m1, d1, i1, v1, vp1, u1, up1, r1,
    t2, tm2, yz, x2, g2, m2, i2, u2, g2h, m2h, d2, i2h, v2, vp2, u2h, up2, r2,
    t3, tm3, u3, g3, m3, d3, i3, v3, vp3, u3h, up3,
    zs, c, cp, a, ap, f2, f1, f0,
    sin, s0, q0, s1, q1, s1u, q1u, sy, qy, sx, qx,
):
    gx, gy, gz = (lax.axis_index(axis) for axis in ("gx", "gy", "gz"))

    inputs = [
        pltpu.make_async_copy(loads, held_loads, sin.at[0]),
        pltpu.make_async_copy(density, held_density, sin.at[1]),
    ]
    for copy in inputs:
        copy.start()

    partners = {(dx, dy, dz) for dx in (-1, 0, 1) for dy in (-1, 0, 1) for dz in (-1, 0, 1)}
    partners |= {(0, dy, dz) for dy, dz in YZ23} | {(dx, 0, 0) for dx in RING}
    partners = sorted(partners - {(0, 0, 0)})
    barrier = pltpu.get_barrier_semaphore()
    for o in partners:
        pl.semaphore_signal(barrier, inc=1, device_id=device(*o), device_id_type=MESH)

    for copy in inputs:
        copy.wait()
    field = rows((8,) + TILE) % 4
    four = [held_loads[0], held_loads[1], held_loads[2], held_density[...]]
    for y in range(4):
        pair = turn_rows(four[3], (3 - y) % 8) if y != 3 else four[3]
        for f in range(3):
            pair = jnp.where(field == f, turn_rows(four[f], (f - y) % 8) if f != y else four[f], pair)
        block[:, y] = pair
        e0[pl.ds(4, 8), y + 4] = pair[:, 0:4]
        e0[pl.ds(4, 8), y + 8] = pair[:, 4:8]
    pl.semaphore_wait(barrier, len(partners))

    span = {-1: (4, 12, 3), 0: (4, 4, 8), 1: (8, 0, 4)}
    sent = []
    copies = []
    for n, (dx, dy) in enumerate(XY8):
        (ax, bx, cx), (ay, by, cy) = span[dx], span[dy]
        copies.append(
            pltpu.make_async_remote_copy(
                src_ref=e0.at[pl.ds(ax, cx), pl.ds(ay, cy)],
                dst_ref=e0.at[pl.ds(bx, cx), pl.ds(by, cy)],
                send_sem=s0.at[n], recv_sem=q0.at[n],
                device_id=device(dx, dy, 0), device_id_type=MESH,
            )
        )
        copies[-1].start()
    k16 = lax.broadcasted_iota(jnp.int32, (16, 128), 0)
    l16 = lax.broadcasted_iota(jnp.int32, (16, 128), 1)
    pick_low = jnp.where((l16 == 128 - ZHALO + k16) & (k16 < ZHALO), 1.0, 0.0).astype(F32)
    pick_high = jnp.where((l16 == k16) & (k16 < ZHALO), 1.0, 0.0).astype(F32)
    n = 8
    for dz, pick in ((-1, pick_high), (1, pick_low)):
        side = 0 if dz > 0 else 1
        for half in (0, 1):
            zsend[side, half] = lax.dot_general(
                pick, block[pl.ds(half * 4, 4)].reshape(128, 128), (((1,), (1,)), ((), ())),
                precision=lax.Precision.HIGHEST, preferred_element_type=F32,
            )
        for dx, dy in itertools.product((-1, 0, 1), repeat=2):
            first, count = {-1: (0, 1), 0: (0, 2), 1: (1, 1)}[dx]
            copies.append(
                pltpu.make_async_remote_copy(
                    src_ref=zsend.at[side, pl.ds(first, count)],
                    dst_ref=zrecv.at[side, 1 - dx, 1 - dy, pl.ds(first, count)],
                    send_sem=s0.at[n], recv_sem=q0.at[n],
                    device_id=device(dx, dy, dz), device_id_type=MESH,
                )
            )
            copies[-1].start()
            n += 1

    def rim2(x):
        m2[x] = jnp.zeros((28,) + TILE, F32)

    loop(0, 28, rim2)
    line = jnp.zeros((10,) + TILE, F32)
    for ref in (m2h, v2, vp2, u2h, up2, r2):
        ref[0] = line
    for ref in (v2, vp2, u2h, up2):
        ref[17] = line
    line = jnp.zeros((6,) + TILE, F32)
    m3[0] = line
    for ref in (v3, vp3, u3h, up3):
        ref[0] = line
        ref[9] = line

    def rim3(x):
        u3[x] = jnp.zeros((16,) + TILE, F32)

    loop(0, 16, rim3)
    for copy in copies:
        copy.wait_recv()
    sent += copies

    low_in, high_in = jnp.where(gz > 0, 1.0, 0.0), jnp.where(gz < SIDE - 1, 1.0, 0.0)
    put = jnp.concatenate([pick_low, pick_high], axis=0)
    for rx, ry in itertools.product((-1, 0, 1), repeat=2):
        inside = None
        if rx:
            inside = gx > 0 if rx < 0 else gx < SIDE - 1
        if ry:
            more = gy > 0 if ry < 0 else gy < SIDE - 1
            inside = more if inside is None else inside & more
        factor = 1.0 if inside is None else jnp.where(inside, 1.0, 0.0)
        for half in {-1: (1,), 0: (0, 1), 1: (0,)}[rx]:
            both = jnp.concatenate([zrecv[0, rx + 1, ry + 1, half], zrecv[1, rx + 1, ry + 1, half]], axis=0)
            ends = lax.dot_general(
                both, put, (((0,), (0,)), ((), ())),
                precision=lax.Precision.HIGHEST, preferred_element_type=F32,
            ).reshape((4, 4) + TILE)
            x_at, nx = 4 + 8 * rx + 4 * half, 3 if rx > 0 else 4
            for late in {-1: (1,), 0: (0, 1), 1: (0,)}[ry]:
                y_at, ny = 4 + 8 * ry + 4 * late, 3 if ry > 0 else 4
                shape = (nx, ny) + TILE
                spot = (pl.ds(x_at, nx), pl.ds(y_at, ny))
                top, lane = rows(shape) < 4, lanes(shape)
                held = ends[0:nx, 0:ny]
                if not late:
                    held = turn_rows(held, 4)
                whole = jnp.where(top, twice(e0[spot]), held)
                dens = jnp.where(top, spread(whole, 3), spread(whole, 7))
                ok = jnp.where(
                    top, 1.0,
                    jnp.where(lane < ZHALO, high_in, jnp.where(lane >= 128 - ZHALO, low_in, 0.0)),
                ) * factor
                g0[spot] = (1.8 * ok) * whole
                m0[spot] = (0.15 * ok) * (0.001 + (1.0 - 0.001) * (dens * dens * dens))

    diagonal(m0, d0, i0, g0, v0, vp0, (1, 15), (1, 14), up_pair, down_pair)
    smooth(v0, vp0, m0, i0, g0, u0, up0, (2, 14), (2, 12), up_pair, down_pair)
    residual(u0, up0, m0, d0, g0, r0, (3, 12), (3, 9), down_pair)
    restrict_xy(r0, t1, 4, 4, 4)
    coarsen_xy(m0, tm1, 4, 4, 4)
    top128 = rows((16,) + TILE) < 4

    def both_ends(tiles, kind):
        flat = tiles[...].reshape(128, 128)
        parts = [product(flat, kind(where)).reshape((16,) + TILE) for where in ("all", "beyond")]
        joined = jnp.where(top128, parts[0], parts[1])
        return joined + turn_rows(joined, 4)

    new_g, new_m = both_ends(t1, restriction), both_ends(tm1, coarsening)
    joined = jnp.where(rows((16,) + TILE) == 3, new_m, new_g)[:, 0:4]
    e1[pl.ds(4, 4), pl.ds(4, 4)] = joined.reshape(4, 4, 4, 128)

    def blocks8(ref, send, recv):
        found = []
        for n, (dx, dy) in enumerate(XY8):
            found.append(
                pltpu.make_async_remote_copy(
                    src_ref=ref.at[pl.ds(4, 4), pl.ds(4, 4)],
                    dst_ref=ref.at[pl.ds({-1: 8, 0: 4, 1: 0}[dx], 4), pl.ds({-1: 8, 0: 4, 1: 0}[dy], 4)],
                    send_sem=send.at[n], recv_sem=recv.at[n],
                    device_id=device(dx, dy, 0), device_id_type=MESH,
                )
            )
        return found

    copies = blocks8(e1, s1, q1)
    for copy in copies:
        copy.start()
    for copy in copies:
        copy.wait_recv()
    sent += copies

    y_index = lax.broadcasted_iota(jnp.int32, (12,) + TILE, 0)
    inside_y = jnp.where(y_index < 4, jnp.where(gy > 0, 1.0, 0.0), jnp.where(y_index < 8, 1.0, jnp.where(gy < SIDE - 1, 1.0, 0.0)))

    def take1(x):
        inside_x = jnp.where(((x >= 4) | (gx > 0)) & ((x < 8) | (gx < SIDE - 1)), 1.0, 0.0)
        whole = twice(e1[x]) * (inside_x * inside_y)
        mod = spread(whole, 3)
        m1[x] = mod
        g1[x] = jnp.where(mod > 0.0, whole, 0.0)

    loop(0, 12, take1)
    diagonal(m1, d1, i1, g1, v1, vp1, (1, 12), (1, 11), up_plain, down_plain)
    smooth(v1, vp1, m1, i1, g1, u1, up1, (2, 9), (2, 7), up_plain, down_plain)
    own = (pl.ds(4, 4), pl.ds(4, 4))
    u1x[own] = u1[own][:, :, 0:4]
    u_copies = blocks8(u1x, s1u, q1u)
    residual(u1, up1, m1, d1, g1, r1, (3, 8), (3, 5), down_plain)
    restrict_xy(r1, t2, 4, 2, 2)
    coarsen_xy(m1, tm2, 4, 2, 2)
    new_g = product(t2[...].reshape(32, 128), restriction("round"))
    new_m = product(tm2[...].reshape(32, 128), coarsening("round"))
    both = jnp.where(rows((32, 128)) % 8 == 3, new_m, new_g).reshape((4,) + TILE)
    group = lanes((4,) + TILE) // 32
    packed = jnp.where(group == 0, spread(both, 0), 0.0)
    for f in (1, 2, 3):
        packed = jnp.where(group == f, spread(turn_lanes(both, 32 * f), f), packed)
    line = packed[0]
    for k in (1, 2, 3):
        line = jnp.where(rows() == k, packed[k], line)
    yz[1, gy] = line[0:4]

    copies = []
    for n, (dy, dz) in enumerate(YZ23):
        copies.append(
            pltpu.make_async_remote_copy(
                src_ref=yz.at[1, gy],
                dst_ref=yz.at[1 - dz, gy],
                send_sem=sy.at[n], recv_sem=qy.at[n],
                device_id=device(0, dy, dz), device_id_type=MESH,
            )
        )
    for copy in copies:
        copy.start()
    for copy in copies:
        copy.wait_recv()
    sent += copies
    shape = (8,) + TILE
    group, field = lanes(shape) // 32, rows(shape) % 4
    is_own = group == field
    is_high, is_low = group == (field + 1) % 4, group == (field + 3) % 4
    low = twice(turn_lanes(yz[0], 96) * low_in)
    own = twice(yz[1])
    high = twice(turn_lanes(yz[2], 32) * high_in)
    columns = []
    for k in range(4):
        whole = jnp.where(is_high, spread(high, k), 0.0)
        whole = jnp.where(is_low, spread(low, k), whole)
        whole = jnp.where(is_own, spread(own, k), whole)
        turned = [whole] + [turn_lanes(whole, 128 - 32 * f) for f in (1, 2, 3)]
        for f in (1, 2, 3):
            whole = jnp.where(field == f, turned[f], whole)
        columns.append(whole)
    for x in range(2):
        for y in range(8):
            x2[2 * gx + x, 2 * y] = columns[2 * x][y, 0:4]
            x2[2 * gx + x, 2 * y + 1] = columns[2 * x + 1][y, 0:4]

    copies = []
    for n, dx in enumerate(RING):
        copies.append(
            pltpu.make_async_remote_copy(
                src_ref=x2.at[pl.ds(2 * gx, 2)],
                dst_ref=x2.at[pl.ds(2 * gx, 2)],
                send_sem=sx.at[n], recv_sem=qx.at[n],
                device_id=device(dx, 0, 0), device_id_type=MESH,
            )
        )
    for copy in copies:
        copy.start()
    for copy in copies:
        copy.wait_recv()
    sent += copies

    for copy in u_copies:
        copy.start()
    sent += u_copies

    def take2(x):
        whole = twice(x2[x])
        mod = spread(whole, 3)
        m2[x + 6, pl.ds(6, 16)] = mod
        g2[x + 6, pl.ds(6, 16)] = jnp.where(mod > 0.0, whole, 0.0)
        whole = jnp.concatenate([x2[x, pl.ds(0, 8)], x2[x, pl.ds(8, 8)]], axis=1)
        mod = jnp.where(rows((8,) + TILE) < 4, spread(whole, 3), spread(whole, 7))
        m2h[x + 1, pl.ds(1, 8)] = mod
        put_rims(m2h, x + 1, mod)
        g2h[x + 1, pl.ds(1, 8)] = jnp.where(mod > 0.0, whole, 0.0)

    loop(0, 16, take2)

    def whole2(ref):
        def store(x, line):
            first, second = halves(line)
            ref[x + 5, pl.ds(6, 8)] = first
            ref[x + 5, pl.ds(14, 8)] = second

        return store

    span = ((1, 17), (1, 8), up_plain, down_plain, True)
    diagonal(m2h, d2, i2h, g2h, v2, vp2, *span, whole2(i2))
    smooth(v2, vp2, m2h, i2h, g2h, u2h, up2, *span, whole2(u2))
    residual(u2h, up2, m2h, d2, g2h, r2, (1, 17), (1, 8), down_plain, True)
    restrict_xy(r2, t3, 1, 8, 4)
    coarsen_xy(m2h, tm3, 1, 8, 4)
    new_g = product(t3[...].reshape(256, 128), restriction("round")).reshape(8, 4, 8, 128)
    new_m = product(tm3[...].reshape(256, 128), coarsening("round")).reshape(8, 4, 8, 128)
    for x in range(8):
        m3[x + 1, pl.ds(1, 4)] = new_m[x]
        put_rims(m3, x + 1, new_m[x])
        g3[x + 1, pl.ds(1, 4)] = jnp.where(new_m[x] > 0.0, new_g[x], 0.0)

    span = ((1, 9), (1, 4), up_plain, down_plain, True)
    diagonal(m3, d3, i3, g3, v3, vp3, *span)

    def two(i):
        smooth(v3, vp3, m3, i3, g3, u3h, up3, *span)
        smooth(u3h, up3, m3, i3, g3, v3, vp3, *span)

    loop_rolled(0, 3, two)

    def whole3(x, line):
        first, second = halves(line)
        u3[x + 3, pl.ds(4, 4)] = first
        u3[x + 3, pl.ds(8, 4)] = second

    smooth(v3, vp3, m3, i3, g3, u3h, up3, *span, whole3)

    x_at, y_at = 2 * gx + 2, 2 * gy + 2
    rise(
        u3[pl.ds(gx + 2, 7), pl.ds(gy + 2, 7)],
        (prolongation("round"),),
        lambda x: u2[x + x_at, pl.ds(y_at, 12)],
        (m2, x_at, y_at), (i2, x_at, y_at), (g2, x_at, y_at),
        zs, c, cp, a, ap, f2, up_plain, down_plain,
    )
    for copy in u_copies:
        copy.wait_recv()
    rise(
        f2[pl.ds(0, 7), pl.ds(0, 7)],
        (prolongation("round"),),
        lambda x: twice(u1x[x]),
        (m1, 0, 0), (i1, 0, 0), (g1, 0, 0),
        zs, c, cp, a, ap, f1, up_plain, down_plain,
    )

    rise(
        f1[pl.ds(1, 7), pl.ds(1, 7)],
        (prolongation("all"), prolongation("beyond")),
        lambda x: u0[x + 2, pl.ds(2, 12)],
        (m0, 2, 2), (i0, 2, 2), (g0, 2, 2),
        zs, c, cp, a, ap, f0, up_pair, down_pair,
    )
    for f in range(3):
        plane = f0[:, f]
        for y in range(8):
            if y != f:
                plane = jnp.where(rows((8,) + TILE) == y, turn_rows(f0[:, y], (y - f) % 8), plane)
        out[f] = plane
    for copy in sent:
        copy.wait_send()


def per_device(loads, density):
    def tiles(*lead):
        return pltpu.VMEM(lead + TILE, F32)

    def thin(*lead):
        return pltpu.VMEM(lead + (4, 128), F32)

    sems = [pltpu.SemaphoreType.DMA((2,))]
    for count in (26, 8, 8, 23, 7):
        sems += [pltpu.SemaphoreType.DMA((count,))] * 2
    return pl.pallas_call(
        kernel,
        out_shape=jax.ShapeDtypeStruct((3,) + (8,) + TILE, F32),
        in_specs=[pl.BlockSpec(memory_space=pl.ANY)] * 2,
        out_specs=pl.BlockSpec(memory_space=pltpu.VMEM),
        scratch_shapes=[tiles(3, 8), tiles(8), tiles(8, 4), thin(15, 15), pltpu.VMEM((2, 2, 16, 128), F32), pltpu.VMEM((2, 3, 3, 2, 16, 128), F32)]
        + [tiles(15, 15)] * 9
        + [tiles(4, 4)] * 2
        + [thin(12, 12)] * 2
        + [tiles(12, 12)] * 9
        + [tiles(2, 2)] * 2
        + [thin(3, 8), thin(16, 16)]
        + [tiles(28, 28)] * 4
        + [tiles(18, 10)] * 9
        + [tiles(8, 4)] * 2
        + [tiles(16, 16)]
        + [tiles(10, 6)] * 8
        + [tiles(7, 7)]
        + [tiles(12, 12)] * 4
        + [tiles(8, 8)] * 3
        + sems,
        compiler_params=pltpu.CompilerParams(
            collective_id=0, has_side_effects=True, vmem_limit_bytes=60 * 2**20
        ),
        cost_estimate=pl.CostEstimate(flops=10**8, bytes_accessed=10**6, transcendentals=0),
    )(loads, density)


def solution(mesh):
    placed = (P(None, "gx", "gy", "gz"), P("gx", "gy", "gz"))
    return jax.shard_map(
        per_device, mesh=mesh, in_specs=placed, out_specs=P(None, "gx", "gy", "gz"), check_vma=False
    )
```

```python
import functools
import itertools

import jax
import jax.numpy as jnp
from jax import lax
from jax.experimental import pallas as pl
from jax.experimental.pallas import tpu as pltpu
from jax.sharding import PartitionSpec as P

MESH = pl.DeviceIdType.MESH
F32 = jnp.float32
TILE = (8, 128)
SIDE = 8
UNROLL = 16
ZHALO = 12
RING = (1, 2, 3, 4, -3, -2, -1)
XY8 = [(dx, dy) for dx in (-1, 0, 1) for dy in (-1, 0, 1) if dx or dy]
YZ23 = [(dy, dz) for dy in (0,) + RING for dz in (-1, 0, 1) if dy or dz]


def around():
    here = [lax.axis_index(axis) for axis in ("gx", "gy", "gz")]
    known = [{0: at} for at in here]

    def device(*steps):
        for at, seen, step in zip(here, known, steps):
            if step % SIDE not in seen:
                seen[step % SIDE] = lax.rem(at + step % SIDE, SIDE)
        return tuple(seen[step % SIDE] for seen, step in zip(known, steps))

    return device


def lanes(shape=TILE):
    return lax.broadcasted_iota(jnp.int32, shape, len(shape) - 1)


def rows(shape=TILE):
    return lax.broadcasted_iota(jnp.int32, shape, len(shape) - 2)


def turn_rows(tiles, by):
    return pltpu.roll(tiles, by, tiles.ndim - 2)


def turn_lanes(tiles, by):
    return pltpu.roll(tiles, by, tiles.ndim - 1)


def up_plain(tiles):
    return turn_lanes(tiles, 127)


def down_plain(tiles):
    return turn_lanes(tiles, 1)


def up_pair(tiles):
    turned = turn_lanes(tiles, 127)
    return jnp.where(lanes(tiles.shape) == 127, turn_rows(turned, 4), turned)


def down_pair(tiles):
    turned = turn_lanes(tiles, 1)
    return jnp.where(lanes(tiles.shape) == 0, turn_rows(turned, 4), turned)


def twice(tiles):
    return jnp.concatenate([tiles, tiles], axis=tiles.ndim - 2)


def spread(tiles, row):
    return jnp.broadcast_to(tiles[..., row : row + 1, :], tiles.shape)


def halves(tiles):
    top, turned = rows(tiles.shape) < 4, turn_rows(tiles, 4)
    return jnp.where(top, tiles, turned), jnp.where(top, turned, tiles)


def put_rims(ref, x, line):
    top, n = rows() < 4, line.shape[0]
    ref[x, 0] = jnp.where(top, 0.0, turn_rows(line[n - 1], 4))
    ref[x, n + 1] = jnp.where(top, turn_rows(line[0], 4), 0.0)


def stencil(v, vp, m, ix, y0, n, mx, my, down):
    wide = pl.ds(y0 - 1, n + 2)
    lower = {sx: v[ix + sx, wide] for sx in (-1, 0, 1)}
    upper = {sx: vp[ix + sx, wide] for sx in (-1, 0, 1)}
    weights = {-1: m[mx - 1, pl.ds(y0 + my - 1, n + 1)], 1: m[mx, pl.ds(y0 + my - 1, n + 1)]}
    above, below = None, None
    for sx in (-1, 1):
        both = lower[sx] + upper[sx]
        for sy in (-1, 1):
            side = slice(1 + sy, 1 + sy + n)
            weight = weights[sx][0:n] if sy < 0 else weights[sx][1 : n + 1]
            hi = weight * (both[side] + (upper[sx][1 : n + 1] + upper[0][side]))
            lo = weight * (both[side] + (lower[sx][1 : n + 1] + lower[0][side]))
            above = hi if above is None else above + hi
            below = lo if below is None else below + lo
    return above + down(below)


def loop(lower, upper, body):
    count = upper - lower
    each = max(k for k in range(1, UNROLL + 1) if count % k == 0)

    def step(i, carry):
        for k in range(each):
            body(lower + i * each + k)
        return carry

    if each == count:
        step(0, 0)
    else:
        lax.fori_loop(0, count // each, step, 0)


def loop_rolled(lower, upper, body):
    def step(i, carry):
        body(i)
        return carry

    lax.fori_loop(lower, upper, step, 0)


def diagonal(m, d4, inv, g, v, vp, xs, ys, up, down, rims=False, also=None):
    y0, n = ys
    at = pl.ds(y0, n)

    def body(x):
        pairs = m[x - 1, pl.ds(y0 - 1, n + 1)] + m[x, pl.ds(y0 - 1, n + 1)]
        four = pairs[0:n] + pairs[1 : n + 1]
        total = four + down(four)
        share = jnp.where(m[x, at] > 0.0, 0.15 / total, 0.0)
        d4[x, at] = 4.0 * total
        inv[x, at] = share
        first = share * g[x, at]
        above = up(first)
        v[x, at] = first
        vp[x, at] = above
        if rims:
            put_rims(v, x, first)
            put_rims(vp, x, above)
        if also is not None:
            also(x, share)

    loop(xs[0], xs[1], body)


def smooth(v, vp, m, inv, g, out, outp, xs, ys, up, down, rims=False, also=None):
    y0, n = ys
    at = pl.ds(y0, n)

    def body(x):
        around = stencil(v, vp, m, x, y0, n, x, 0, down)
        new = 0.4 * v[x, at] + inv[x, at] * (g[x, at] + around)
        above = up(new)
        out[x, at] = new
        outp[x, at] = above
        if rims:
            put_rims(out, x, new)
            put_rims(outp, x, above)
        if also is not None:
            also(x, new)

    loop(xs[0], xs[1], body)


def residual(v, vp, m, d4, g, out, xs, ys, down, rims=False):
    y0, n = ys
    at = pl.ds(y0, n)

    def body(x):
        around = stencil(v, vp, m, x, y0, n, x, 0, down)
        left = (g[x, at] - d4[x, at] * v[x, at]) + around
        out[x, at] = left
        if rims:
            put_rims(out, x, left)

    loop(xs[0], xs[1], body)


def restrict_xy(res, out, base, count_x, count):
    def body(i):
        x = base + 2 * i
        wide = pl.ds(base - 1, 2 * count + 1)
        line = res[x, wide] + 0.5 * (res[x - 1, wide] + res[x + 1, wide])
        for k in range(count):
            out[i, k] = line[2 * k + 1] + 0.5 * (line[2 * k] + line[2 * k + 2])

    loop(0, count_x, body)


def coarsen_xy(m, out, base, count_x, count):
    def body(i):
        x = base + 2 * i
        wide = pl.ds(base, 2 * count)
        line = m[x, wide] + m[x + 1, wide]
        for k in range(count):
            out[i, k] = line[2 * k] + line[2 * k + 1]

    loop(0, count_x, body)


def place(index, own):
    if own == "all":
        return index
    if own == "beyond":
        return jnp.where(index < 64, index + 128, index - 128)
    return jnp.where(index < 96, index, index - 128)


def restriction(fine):
    f = place(lax.broadcasted_iota(jnp.int32, (128, 128), 0), fine)
    c = place(lax.broadcasted_iota(jnp.int32, (128, 128), 1), "round")
    gap = f - 2 * c
    return jnp.where(gap == 0, 0.5, jnp.where((gap == 1) | (gap == -1), 0.25, 0.0)).astype(F32)


def coarsening(fine):
    f = place(lax.broadcasted_iota(jnp.int32, (128, 128), 0), fine)
    c = place(lax.broadcasted_iota(jnp.int32, (128, 128), 1), "round")
    gap = f - 2 * c
    return jnp.where((gap == 0) | (gap == 1), 0.125, 0.0).astype(F32)


def prolongation(fine):
    c = place(lax.broadcasted_iota(jnp.int32, (128, 128), 0), "round")
    f = place(lax.broadcasted_iota(jnp.int32, (128, 128), 1), fine)
    gap = f - 2 * c
    return jnp.where(gap == 0, 1.0, jnp.where((gap == 1) | (gap == -1), 0.5, 0.0)).astype(F32)


def product(a, b):
    return jnp.dot(a, b, precision=lax.Precision.HIGHEST, preferred_element_type=F32)


def rise(source, mats, before, m, inv, g, zs, c, cp, a, ap, out, up, down):
    flat = source.reshape(7 * 7 * 8, 128)
    wide = product(flat, mats[0])
    if len(mats) == 2:
        top = lax.broadcasted_iota(jnp.int32, (7 * 7 * 8, 128), 0) % 8 < 4
        wide = jnp.where(top, wide, product(flat, mats[1]))
    zs[...] = wide.reshape(7, 7, 8, 128)
    m_ref, mx, my = m
    i_ref, ix, iy = inv
    g_ref, gx, gy = g

    def correct(i):
        for half in (0, 1):
            x = 2 * i + half
            line = zs[i] if half == 0 else 0.5 * (zs[i] + zs[i + 1])
            middle = 0.5 * (line[0:6] + line[1:7])
            add = jnp.stack([line[0:6], middle], axis=1).reshape((12,) + TILE)
            new = jnp.where(m_ref[x + mx, pl.ds(my, 12)] > 0.0, before(x) + add, 0.0)
            c[x] = new
            cp[x] = up(new)

    loop(0, 6, correct)

    def sweep(old, oldp, x, y0, n):
        around = stencil(old, oldp, m_ref, x, y0, n, x + mx, my, down)
        new = 0.4 * old[x, pl.ds(y0, n)] + i_ref[x + ix, pl.ds(y0 + iy, n)] * (
            g_ref[x + gx, pl.ds(y0 + gy, n)] + around
        )
        return jnp.where(m_ref[x + mx, pl.ds(y0 + my, n)] > 0.0, new, 0.0)

    def sweep_a(x):
        new = sweep(c, cp, x, 1, 10)
        a[x, pl.ds(1, 10)] = new
        ap[x, pl.ds(1, 10)] = up(new)

    loop(1, 11, sweep_a)

    def sweep_b(x):
        out[x - 2] = sweep(a, ap, x, 2, 8)

    loop(2, 10, sweep_b)


def kernel(
    loads, density, out, held_loads, held_density, block, e0, zsend, zrecv, g0, m0, d0, i0, v0, vp0, u0, up0, r0,
    t1, tm1, e1, u1x, g1, m1, d1, i1, v1, vp1, u1, up1, r1,
    t2, tm2, yz, x2, g2, m2, i2, u2, g2h, m2h, d2, i2h, v2, vp2, u2h, up2, r2,
    t3, tm3, u3, g3, m3, d3, i3, v3, vp3, u3h, up3,
    zs, c, cp, a, ap, f2, f1, f0,
    sin, s0, q0, s1, q1, s1u, q1u, sy, qy, sx, qx,
):
    device = around()
    gx, gy, gz = device(0, 0, 0)

    inputs = [
        pltpu.make_async_copy(loads, held_loads, sin.at[0]),
        pltpu.make_async_copy(density, held_density, sin.at[1]),
    ]
    for copy in inputs:
        copy.start()
    for step in RING:
        device(step, step, step)

    partners = {(dx, dy, dz) for dx in (-1, 0, 1) for dy in (-1, 0, 1) for dz in (-1, 0, 1)}
    partners |= {(0, dy, dz) for dy, dz in YZ23} | {(dx, 0, 0) for dx in RING}
    partners = sorted(partners - {(0, 0, 0)})
    barrier = pltpu.get_barrier_semaphore()
    for o in partners:
        pl.semaphore_signal(barrier, inc=1, device_id=device(*o), device_id_type=MESH)

    for copy in inputs:
        copy.wait()
    field = rows((8,) + TILE) % 4
    four = [held_loads[0], held_loads[1], held_loads[2], held_density[...]]
    for y in range(4):
        pair = turn_rows(four[3], (3 - y) % 8) if y != 3 else four[3]
        for f in range(3):
            pair = jnp.where(field == f, turn_rows(four[f], (f - y) % 8) if f != y else four[f], pair)
        block[:, y] = pair
        e0[pl.ds(4, 8), y + 4] = pair[:, 0:4]
        e0[pl.ds(4, 8), y + 8] = pair[:, 4:8]
    k16 = lax.broadcasted_iota(jnp.int32, (16, 128), 0)
    l16 = lax.broadcasted_iota(jnp.int32, (16, 128), 1)
    pick_low = jnp.where((l16 == 128 - ZHALO + k16) & (k16 < ZHALO), 1.0, 0.0).astype(F32)
    pick_high = jnp.where((l16 == k16) & (k16 < ZHALO), 1.0, 0.0).astype(F32)
    for side, pick in enumerate((pick_low, pick_high)):
        for half in (0, 1):
            zsend[side, half] = lax.dot_general(
                pick, block[pl.ds(half * 4, 4)].reshape(128, 128), (((1,), (1,)), ((), ())),
                precision=lax.Precision.HIGHEST, preferred_element_type=F32,
            )
    pl.semaphore_wait(barrier, len(partners))

    span = {-1: (4, 12, 3), 0: (4, 4, 8), 1: (8, 0, 4)}
    sent = []
    copies = []
    for n, (dx, dy) in enumerate(XY8):
        (ax, bx, cx), (ay, by, cy) = span[dx], span[dy]
        copies.append(
            pltpu.make_async_remote_copy(
                src_ref=e0.at[pl.ds(ax, cx), pl.ds(ay, cy)],
                dst_ref=e0.at[pl.ds(bx, cx), pl.ds(by, cy)],
                send_sem=s0.at[n], recv_sem=q0.at[n],
                device_id=device(dx, dy, 0), device_id_type=MESH,
            )
        )
        copies[-1].start()
    n = 8
    for dz in (-1, 1):
        side = 0 if dz > 0 else 1
        for dx, dy in itertools.product((-1, 0, 1), repeat=2):
            first, count = {-1: (0, 1), 0: (0, 2), 1: (1, 1)}[dx]
            copies.append(
                pltpu.make_async_remote_copy(
                    src_ref=zsend.at[side, pl.ds(first, count)],
                    dst_ref=zrecv.at[side, 1 - dx, 1 - dy, pl.ds(first, count)],
                    send_sem=s0.at[n], recv_sem=q0.at[n],
                    device_id=device(dx, dy, dz), device_id_type=MESH,
                )
            )
            copies[-1].start()
            n += 1

    def rim2(x):
        m2[x] = jnp.zeros((28,) + TILE, F32)

    loop(0, 28, rim2)
    line = jnp.zeros((10,) + TILE, F32)
    for ref in (m2h, v2, vp2, u2h, up2, r2):
        ref[0] = line
    for ref in (v2, vp2, u2h, up2):
        ref[17] = line
    line = jnp.zeros((6,) + TILE, F32)
    m3[0] = line
    for ref in (v3, vp3, u3h, up3):
        ref[0] = line
        ref[9] = line

    def rim3(x):
        u3[x] = jnp.zeros((16,) + TILE, F32)

    loop(0, 16, rim3)
    for copy in copies:
        copy.wait_recv()
    sent += copies

    low_in, high_in = jnp.where(gz > 0, 1.0, 0.0), jnp.where(gz < SIDE - 1, 1.0, 0.0)
    put = jnp.concatenate([pick_low, pick_high], axis=0)
    for rx, ry in [(0, 0), (0, -1), (0, 1), (-1, 0), (1, 0), (-1, -1), (-1, 1), (1, -1), (1, 1)]:
        inside = None
        if rx:
            inside = gx > 0 if rx < 0 else gx < SIDE - 1
        if ry:
            more = gy > 0 if ry < 0 else gy < SIDE - 1
            inside = more if inside is None else inside & more
        factor = 1.0 if inside is None else jnp.where(inside, 1.0, 0.0)
        for half in {-1: (1,), 0: (0, 1), 1: (0,)}[rx]:
            both = jnp.concatenate([zrecv[0, rx + 1, ry + 1, half], zrecv[1, rx + 1, ry + 1, half]], axis=0)
            ends = lax.dot_general(
                both, put, (((0,), (0,)), ((), ())),
                precision=lax.Precision.HIGHEST, preferred_element_type=F32,
            ).reshape((4, 4) + TILE)
            x_at, nx = 4 + 8 * rx + 4 * half, 3 if rx > 0 else 4
            for late in {-1: (1,), 0: (0, 1), 1: (0,)}[ry]:
                y_at, ny = 4 + 8 * ry + 4 * late, 3 if ry > 0 else 4
                shape = (nx, ny) + TILE
                spot = (pl.ds(x_at, nx), pl.ds(y_at, ny))
                top, lane = rows(shape) < 4, lanes(shape)
                held = ends[0:nx, 0:ny]
                if not late:
                    held = turn_rows(held, 4)
                whole = jnp.where(top, twice(e0[spot]), held)
                dens = jnp.where(top, spread(whole, 3), spread(whole, 7))
                ok = jnp.where(
                    top, 1.0,
                    jnp.where(lane < ZHALO, high_in, jnp.where(lane >= 128 - ZHALO, low_in, 0.0)),
                ) * factor
                g0[spot] = (1.8 * ok) * whole
                m0[spot] = (0.15 * ok) * (0.001 + (1.0 - 0.001) * (dens * dens * dens))

    diagonal(m0, d0, i0, g0, v0, vp0, (1, 15), (1, 14), up_pair, down_pair)
    smooth(v0, vp0, m0, i0, g0, u0, up0, (2, 14), (2, 12), up_pair, down_pair)
    residual(u0, up0, m0, d0, g0, r0, (3, 12), (3, 9), down_pair)
    restrict_xy(r0, t1, 4, 4, 4)
    coarsen_xy(m0, tm1, 4, 4, 4)
    top128 = rows((16,) + TILE) < 4

    def both_ends(tiles, kind):
        flat = tiles[...].reshape(128, 128)
        parts = [product(flat, kind(where)).reshape((16,) + TILE) for where in ("all", "beyond")]
        joined = jnp.where(top128, parts[0], parts[1])
        return joined + turn_rows(joined, 4)

    new_g, new_m = both_ends(t1, restriction), both_ends(tm1, coarsening)
    joined = jnp.where(rows((16,) + TILE) == 3, new_m, new_g)[:, 0:4]
    e1[pl.ds(4, 4), pl.ds(4, 4)] = joined.reshape(4, 4, 4, 128)

    def blocks8(ref, send, recv):
        found = []
        for n, (dx, dy) in enumerate(XY8):
            found.append(
                pltpu.make_async_remote_copy(
                    src_ref=ref.at[pl.ds(4, 4), pl.ds(4, 4)],
                    dst_ref=ref.at[pl.ds({-1: 8, 0: 4, 1: 0}[dx], 4), pl.ds({-1: 8, 0: 4, 1: 0}[dy], 4)],
                    send_sem=send.at[n], recv_sem=recv.at[n],
                    device_id=device(dx, dy, 0), device_id_type=MESH,
                )
            )
        return found

    copies = blocks8(e1, s1, q1)
    for copy in copies:
        copy.start()
    for copy in copies:
        copy.wait_recv()
    sent += copies

    y_index = lax.broadcasted_iota(jnp.int32, (12,) + TILE, 0)
    inside_y = jnp.where(y_index < 4, jnp.where(gy > 0, 1.0, 0.0), jnp.where(y_index < 8, 1.0, jnp.where(gy < SIDE - 1, 1.0, 0.0)))

    def take1(x):
        inside_x = jnp.where(((x >= 4) | (gx > 0)) & ((x < 8) | (gx < SIDE - 1)), 1.0, 0.0)
        whole = twice(e1[x]) * (inside_x * inside_y)
        mod = spread(whole, 3)
        m1[x] = mod
        g1[x] = jnp.where(mod > 0.0, whole, 0.0)

    loop(0, 12, take1)
    diagonal(m1, d1, i1, g1, v1, vp1, (1, 12), (1, 11), up_plain, down_plain)
    smooth(v1, vp1, m1, i1, g1, u1, up1, (2, 9), (2, 7), up_plain, down_plain)
    own = (pl.ds(4, 4), pl.ds(4, 4))
    u1x[own] = u1[own][:, :, 0:4]
    u_copies = blocks8(u1x, s1u, q1u)
    residual(u1, up1, m1, d1, g1, r1, (3, 8), (3, 5), down_plain)
    restrict_xy(r1, t2, 4, 2, 2)
    coarsen_xy(m1, tm2, 4, 2, 2)
    new_g = product(t2[...].reshape(32, 128), restriction("round"))
    new_m = product(tm2[...].reshape(32, 128), coarsening("round"))
    both = jnp.where(rows((32, 128)) % 8 == 3, new_m, new_g).reshape((4,) + TILE)
    group = lanes((4,) + TILE) // 32
    packed = jnp.where(group == 0, spread(both, 0), 0.0)
    for f in (1, 2, 3):
        packed = jnp.where(group == f, spread(turn_lanes(both, 32 * f), f), packed)
    line = packed[0]
    for k in (1, 2, 3):
        line = jnp.where(rows() == k, packed[k], line)
    yz[1, gy] = line[0:4]

    copies = []
    for n, (dy, dz) in enumerate(YZ23):
        copies.append(
            pltpu.make_async_remote_copy(
                src_ref=yz.at[1, gy],
                dst_ref=yz.at[1 - dz, gy],
                send_sem=sy.at[n], recv_sem=qy.at[n],
                device_id=device(0, dy, dz), device_id_type=MESH,
            )
        )
    for copy in copies:
        copy.start()
    for copy in copies:
        copy.wait_recv()
    sent += copies
    shape = (8,) + TILE
    group, field = lanes(shape) // 32, rows(shape) % 4
    is_own = group == field
    is_high, is_low = group == (field + 1) % 4, group == (field + 3) % 4
    low = twice(turn_lanes(yz[0], 96) * low_in)
    own = twice(yz[1])
    high = twice(turn_lanes(yz[2], 32) * high_in)
    columns = []
    for k in range(4):
        whole = jnp.where(is_high, spread(high, k), 0.0)
        whole = jnp.where(is_low, spread(low, k), whole)
        whole = jnp.where(is_own, spread(own, k), whole)
        turned = [whole] + [turn_lanes(whole, 128 - 32 * f) for f in (1, 2, 3)]
        for f in (1, 2, 3):
            whole = jnp.where(field == f, turned[f], whole)
        columns.append(whole)
    for x in range(2):
        for y in range(8):
            x2[2 * gx + x, 2 * y] = columns[2 * x][y, 0:4]
            x2[2 * gx + x, 2 * y + 1] = columns[2 * x + 1][y, 0:4]

    copies = []
    for n, dx in enumerate(RING):
        copies.append(
            pltpu.make_async_remote_copy(
                src_ref=x2.at[pl.ds(2 * gx, 2)],
                dst_ref=x2.at[pl.ds(2 * gx, 2)],
                send_sem=sx.at[n], recv_sem=qx.at[n],
                device_id=device(dx, 0, 0), device_id_type=MESH,
            )
        )
    for copy in copies:
        copy.start()
    for copy in copies:
        copy.wait_recv()
    sent += copies

    for copy in u_copies:
        copy.start()
    sent += u_copies

    def take2(x):
        whole = twice(x2[x])
        mod = spread(whole, 3)
        m2[x + 6, pl.ds(6, 16)] = mod
        g2[x + 6, pl.ds(6, 16)] = jnp.where(mod > 0.0, whole, 0.0)
        whole = jnp.concatenate([x2[x, pl.ds(0, 8)], x2[x, pl.ds(8, 8)]], axis=1)
        mod = jnp.where(rows((8,) + TILE) < 4, spread(whole, 3), spread(whole, 7))
        m2h[x + 1, pl.ds(1, 8)] = mod
        put_rims(m2h, x + 1, mod)
        g2h[x + 1, pl.ds(1, 8)] = jnp.where(mod > 0.0, whole, 0.0)

    loop(0, 16, take2)

    def whole2(ref):
        def store(x, line):
            first, second = halves(line)
            ref[x + 5, pl.ds(6, 8)] = first
            ref[x + 5, pl.ds(14, 8)] = second

        return store

    span = ((1, 17), (1, 8), up_plain, down_plain, True)
    diagonal(m2h, d2, i2h, g2h, v2, vp2, *span, whole2(i2))
    smooth(v2, vp2, m2h, i2h, g2h, u2h, up2, *span, whole2(u2))
    residual(u2h, up2, m2h, d2, g2h, r2, (1, 17), (1, 8), down_plain, True)
    restrict_xy(r2, t3, 1, 8, 4)
    coarsen_xy(m2h, tm3, 1, 8, 4)
    new_g = product(t3[...].reshape(256, 128), restriction("round")).reshape(8, 4, 8, 128)
    new_m = product(tm3[...].reshape(256, 128), coarsening("round")).reshape(8, 4, 8, 128)
    for x in range(8):
        m3[x + 1, pl.ds(1, 4)] = new_m[x]
        put_rims(m3, x + 1, new_m[x])
        g3[x + 1, pl.ds(1, 4)] = jnp.where(new_m[x] > 0.0, new_g[x], 0.0)

    span = ((1, 9), (1, 4), up_plain, down_plain, True)
    diagonal(m3, d3, i3, g3, v3, vp3, *span)

    def two(i):
        smooth(v3, vp3, m3, i3, g3, u3h, up3, *span)
        smooth(u3h, up3, m3, i3, g3, v3, vp3, *span)

    loop_rolled(0, 3, two)

    def whole3(x, line):
        first, second = halves(line)
        u3[x + 3, pl.ds(4, 4)] = first
        u3[x + 3, pl.ds(8, 4)] = second

    smooth(v3, vp3, m3, i3, g3, u3h, up3, *span, whole3)

    x_at, y_at = 2 * gx + 2, 2 * gy + 2
    rise(
        u3[pl.ds(gx + 2, 7), pl.ds(gy + 2, 7)],
        (prolongation("round"),),
        lambda x: u2[x + x_at, pl.ds(y_at, 12)],
        (m2, x_at, y_at), (i2, x_at, y_at), (g2, x_at, y_at),
        zs, c, cp, a, ap, f2, up_plain, down_plain,
    )
    for copy in u_copies:
        copy.wait_recv()
    rise(
        f2[pl.ds(0, 7), pl.ds(0, 7)],
        (prolongation("round"),),
        lambda x: twice(u1x[x]),
        (m1, 0, 0), (i1, 0, 0), (g1, 0, 0),
        zs, c, cp, a, ap, f1, up_plain, down_plain,
    )

    rise(
        f1[pl.ds(1, 7), pl.ds(1, 7)],
        (prolongation("all"), prolongation("beyond")),
        lambda x: u0[x + 2, pl.ds(2, 12)],
        (m0, 2, 2), (i0, 2, 2), (g0, 2, 2),
        zs, c, cp, a, ap, f0, up_pair, down_pair,
    )
    for f in range(3):
        plane = f0[:, f]
        for y in range(8):
            if y != f:
                plane = jnp.where(rows((8,) + TILE) == y, turn_rows(f0[:, y], (y - f) % 8), plane)
        out[f] = plane
    for copy in sent:
        copy.wait_send()


def per_device(loads, density):
    def tiles(*lead):
        return pltpu.VMEM(lead + TILE, F32)

    def thin(*lead):
        return pltpu.VMEM(lead + (4, 128), F32)

    sems = [pltpu.SemaphoreType.DMA((2,))]
    for count in (26, 8, 8, 23, 7):
        sems += [pltpu.SemaphoreType.DMA((count,))] * 2
    return pl.pallas_call(
        kernel,
        out_shape=jax.ShapeDtypeStruct((3,) + (8,) + TILE, F32),
        in_specs=[pl.BlockSpec(memory_space=pl.ANY)] * 2,
        out_specs=pl.BlockSpec(memory_space=pltpu.VMEM),
        scratch_shapes=[tiles(3, 8), tiles(8), tiles(8, 4), thin(15, 15), pltpu.VMEM((2, 2, 16, 128), F32), pltpu.VMEM((2, 3, 3, 2, 16, 128), F32)]
        + [tiles(15, 15)] * 9
        + [tiles(4, 4)] * 2
        + [thin(12, 12)] * 2
        + [tiles(12, 12)] * 9
        + [tiles(2, 2)] * 2
        + [thin(3, 8), thin(16, 16)]
        + [tiles(28, 28)] * 4
        + [tiles(18, 10)] * 9
        + [tiles(8, 4)] * 2
        + [tiles(16, 16)]
        + [tiles(10, 6)] * 8
        + [tiles(7, 7)]
        + [tiles(12, 12)] * 4
        + [tiles(8, 8)] * 3
        + sems,
        compiler_params=pltpu.CompilerParams(
            collective_id=0, has_side_effects=True, vmem_limit_bytes=60 * 2**20
        ),
        cost_estimate=pl.CostEstimate(flops=10**8, bytes_accessed=10**6, transcendentals=0),
    )(loads, density)


def solution(mesh):
    placed = (P(None, "gx", "gy", "gz"), P("gx", "gy", "gz"))
    return jax.shard_map(
        per_device, mesh=mesh, in_specs=placed, out_specs=P(None, "gx", "gy", "gz"), check_vma=False
    )
```

```python
import functools
import itertools

import jax
import jax.numpy as jnp
from jax import lax
from jax.experimental import pallas as pl
from jax.experimental.pallas import tpu as pltpu
from jax.sharding import PartitionSpec as P

MESH = pl.DeviceIdType.MESH
F32 = jnp.float32
TILE = (8, 128)
SIDE = 8
UNROLL = 16
ZHALO = 12
RING = (1, 2, 3, 4, -3, -2, -1)
XY8 = [(dx, dy) for dx in (-1, 0, 1) for dy in (-1, 0, 1) if dx or dy]
YZ23 = [(dy, dz) for dy in (0,) + RING for dz in (-1, 0, 1) if dy or dz]


def around():
    here = [lax.axis_index(axis) for axis in ("gx", "gy", "gz")]
    known = [{0: at} for at in here]

    def device(*steps):
        for at, seen, step in zip(here, known, steps):
            if step % SIDE not in seen:
                seen[step % SIDE] = lax.rem(at + step % SIDE, SIDE)
        return tuple(seen[step % SIDE] for seen, step in zip(known, steps))

    return device


def lanes(shape=TILE):
    return lax.broadcasted_iota(jnp.int32, shape, len(shape) - 1)


def rows(shape=TILE):
    return lax.broadcasted_iota(jnp.int32, shape, len(shape) - 2)


def turn_rows(tiles, by):
    return pltpu.roll(tiles, by, tiles.ndim - 2)


def turn_lanes(tiles, by):
    return pltpu.roll(tiles, by, tiles.ndim - 1)


def up_plain(tiles):
    return turn_lanes(tiles, 127)


def down_plain(tiles):
    return turn_lanes(tiles, 1)


def up_pair(tiles):
    turned = turn_lanes(tiles, 127)
    return jnp.where(lanes(tiles.shape) == 127, turn_rows(turned, 4), turned)


def down_pair(tiles):
    turned = turn_lanes(tiles, 1)
    return jnp.where(lanes(tiles.shape) == 0, turn_rows(turned, 4), turned)


def twice(tiles):
    return jnp.concatenate([tiles, tiles], axis=tiles.ndim - 2)


def spread(tiles, row):
    return jnp.broadcast_to(tiles[..., row : row + 1, :], tiles.shape)


def halves(tiles):
    top, turned = rows(tiles.shape) < 4, turn_rows(tiles, 4)
    return jnp.where(top, tiles, turned), jnp.where(top, turned, tiles)


def put_rims(ref, x, line):
    top, n = rows() < 4, line.shape[0]
    ref[x, 0] = jnp.where(top, 0.0, turn_rows(line[n - 1], 4))
    ref[x, n + 1] = jnp.where(top, turn_rows(line[0], 4), 0.0)


def stencil(v, vp, m, ix, y0, n, mx, my, down):
    wide = pl.ds(y0 - 1, n + 2)
    lower = {sx: v[ix + sx, wide] for sx in (-1, 0, 1)}
    upper = {sx: vp[ix + sx, wide] for sx in (-1, 0, 1)}
    weights = {-1: m[mx - 1, pl.ds(y0 + my - 1, n + 1)], 1: m[mx, pl.ds(y0 + my - 1, n + 1)]}
    above, below = None, None
    for sx in (-1, 1):
        both = lower[sx] + upper[sx]
        for sy in (-1, 1):
            side = slice(1 + sy, 1 + sy + n)
            weight = weights[sx][0:n] if sy < 0 else weights[sx][1 : n + 1]
            hi = weight * (both[side] + (upper[sx][1 : n + 1] + upper[0][side]))
            lo = weight * (both[side] + (lower[sx][1 : n + 1] + lower[0][side]))
            above = hi if above is None else above + hi
            below = lo if below is None else below + lo
    return above + down(below)


def loop(lower, upper, body):
    count = upper - lower
    each = max(k for k in range(1, UNROLL + 1) if count % k == 0)

    def step(i, carry):
        for k in range(each):
            body(lower + i * each + k)
        return carry

    if each == count:
        step(0, 0)
    else:
        lax.fori_loop(0, count // each, step, 0)


def loop_rolled(lower, upper, body):
    def step(i, carry):
        body(i)
        return carry

    lax.fori_loop(lower, upper, step, 0)


def diagonal(m, d4, inv, xs, ys, down, also=None):
    y0, n = ys
    at = pl.ds(y0, n)

    def body(x):
        pairs = m[x - 1, pl.ds(y0 - 1, n + 1)] + m[x, pl.ds(y0 - 1, n + 1)]
        four = pairs[0:n] + pairs[1 : n + 1]
        total = four + down(four)
        share = jnp.where(m[x, at] > 0.0, 0.15 / total, 0.0)
        d4[x, at] = 4.0 * total
        inv[x, at] = share
        if also is not None:
            also(x, share)

    loop(xs[0], xs[1], body)


def first_sweep(inv, g, v, vp, xs, ys, up, rims=False):
    y0, n = ys
    at = pl.ds(y0, n)

    def body(x):
        first = inv[x, at] * g[x, at]
        above = up(first)
        v[x, at] = first
        vp[x, at] = above
        if rims:
            put_rims(v, x, first)
            put_rims(vp, x, above)

    loop(xs[0], xs[1], body)


def smooth(v, vp, m, inv, g, out, outp, xs, ys, up, down, rims=False, also=None):
    y0, n = ys
    at = pl.ds(y0, n)

    def body(x):
        around = stencil(v, vp, m, x, y0, n, x, 0, down)
        new = 0.4 * v[x, at] + inv[x, at] * (g[x, at] + around)
        above = up(new)
        out[x, at] = new
        outp[x, at] = above
        if rims:
            put_rims(out, x, new)
            put_rims(outp, x, above)
        if also is not None:
            also(x, new)

    loop(xs[0], xs[1], body)


def residual(v, vp, m, d4, g, out, xs, ys, down, rims=False):
    y0, n = ys
    at = pl.ds(y0, n)

    def body(x):
        around = stencil(v, vp, m, x, y0, n, x, 0, down)
        left = (g[x, at] - d4[x, at] * v[x, at]) + around
        out[x, at] = left
        if rims:
            put_rims(out, x, left)

    loop(xs[0], xs[1], body)


def restrict_xy(res, out, base, count_x, count):
    def body(i):
        x = base + 2 * i
        wide = pl.ds(base - 1, 2 * count + 1)
        line = res[x, wide] + 0.5 * (res[x - 1, wide] + res[x + 1, wide])
        for k in range(count):
            out[i, k] = line[2 * k + 1] + 0.5 * (line[2 * k] + line[2 * k + 2])

    loop(0, count_x, body)


def coarsen_xy(m, out, base, count_x, count):
    def body(i):
        x = base + 2 * i
        wide = pl.ds(base, 2 * count)
        line = m[x, wide] + m[x + 1, wide]
        for k in range(count):
            out[i, k] = line[2 * k] + line[2 * k + 1]

    loop(0, count_x, body)


def place(index, own):
    if own == "all":
        return index
    if own == "beyond":
        return jnp.where(index < 64, index + 128, index - 128)
    return jnp.where(index < 96, index, index - 128)


def restriction(fine):
    f = place(lax.broadcasted_iota(jnp.int32, (128, 128), 0), fine)
    c = place(lax.broadcasted_iota(jnp.int32, (128, 128), 1), "round")
    gap = f - 2 * c
    return jnp.where(gap == 0, 0.5, jnp.where((gap == 1) | (gap == -1), 0.25, 0.0)).astype(F32)


def coarsening(fine):
    f = place(lax.broadcasted_iota(jnp.int32, (128, 128), 0), fine)
    c = place(lax.broadcasted_iota(jnp.int32, (128, 128), 1), "round")
    gap = f - 2 * c
    return jnp.where((gap == 0) | (gap == 1), 0.125, 0.0).astype(F32)


def prolongation(fine):
    c = place(lax.broadcasted_iota(jnp.int32, (128, 128), 0), "round")
    f = place(lax.broadcasted_iota(jnp.int32, (128, 128), 1), fine)
    gap = f - 2 * c
    return jnp.where(gap == 0, 1.0, jnp.where((gap == 1) | (gap == -1), 0.5, 0.0)).astype(F32)


def product(a, b):
    return jnp.dot(a, b, precision=lax.Precision.HIGHEST, preferred_element_type=F32)


def rise(source, mats, before, m, inv, g, zs, c, cp, a, ap, out, up, down):
    flat = source.reshape(7 * 7 * 8, 128)
    wide = product(flat, mats[0])
    if len(mats) == 2:
        top = lax.broadcasted_iota(jnp.int32, (7 * 7 * 8, 128), 0) % 8 < 4
        wide = jnp.where(top, wide, product(flat, mats[1]))
    zs[...] = wide.reshape(7, 7, 8, 128)
    m_ref, mx, my = m
    i_ref, ix, iy = inv
    g_ref, gx, gy = g

    def correct(i):
        for half in (0, 1):
            x = 2 * i + half
            line = zs[i] if half == 0 else 0.5 * (zs[i] + zs[i + 1])
            middle = 0.5 * (line[0:6] + line[1:7])
            add = jnp.stack([line[0:6], middle], axis=1).reshape((12,) + TILE)
            new = jnp.where(m_ref[x + mx, pl.ds(my, 12)] > 0.0, before(x) + add, 0.0)
            c[x] = new
            cp[x] = up(new)

    loop(0, 6, correct)

    def sweep(old, oldp, x, y0, n):
        around = stencil(old, oldp, m_ref, x, y0, n, x + mx, my, down)
        new = 0.4 * old[x, pl.ds(y0, n)] + i_ref[x + ix, pl.ds(y0 + iy, n)] * (
            g_ref[x + gx, pl.ds(y0 + gy, n)] + around
        )
        return jnp.where(m_ref[x + mx, pl.ds(y0 + my, n)] > 0.0, new, 0.0)

    def sweep_a(x):
        new = sweep(c, cp, x, 1, 10)
        a[x, pl.ds(1, 10)] = new
        ap[x, pl.ds(1, 10)] = up(new)

    loop(1, 11, sweep_a)

    def sweep_b(x):
        out[x - 2] = sweep(a, ap, x, 2, 8)

    loop(2, 10, sweep_b)


def kernel(
    loads, density, out, held_loads, held_density, block, e0, zsend, zrecv, g0, m0, d0, i0, v0, vp0, u0, up0, r0,
    t1, tm1, e1, u1x, g1, m1, d1, i1, v1, vp1, u1, up1, r1,
    t2, yz, yzm, xm, x2, g2, m2, i2, u2, g2h, m2h, d2, i2h, v2, vp2, u2h, up2, r2,
    t3, tm3, u3, g3, m3, d3, i3, v3, vp3, u3h, up3,
    zs, c, cp, a, ap, f2, f1, f0,
    sin, s0, q0, s1, q1, s1u, q1u, sy, qy, sx, qx, sym, qym, sxm, qxm,
):
    device = around()
    gx, gy, gz = device(0, 0, 0)

    inputs = [
        pltpu.make_async_copy(loads, held_loads, sin.at[0]),
        pltpu.make_async_copy(density, held_density, sin.at[1]),
    ]
    for copy in inputs:
        copy.start()
    for step in RING:
        device(step, step, step)

    partners = {(dx, dy, dz) for dx in (-1, 0, 1) for dy in (-1, 0, 1) for dz in (-1, 0, 1)}
    partners |= {(0, dy, dz) for dy, dz in YZ23} | {(dx, 0, 0) for dx in RING}
    partners = sorted(partners - {(0, 0, 0)})
    barrier = pltpu.get_barrier_semaphore()
    for o in partners:
        pl.semaphore_signal(barrier, inc=1, device_id=device(*o), device_id_type=MESH)

    for copy in inputs:
        copy.wait()
    field = rows((8,) + TILE) % 4
    four = [held_loads[0], held_loads[1], held_loads[2], held_density[...]]
    for y in range(4):
        pair = turn_rows(four[3], (3 - y) % 8) if y != 3 else four[3]
        for f in range(3):
            pair = jnp.where(field == f, turn_rows(four[f], (f - y) % 8) if f != y else four[f], pair)
        block[:, y] = pair
        e0[pl.ds(4, 8), y + 4] = pair[:, 0:4]
        e0[pl.ds(4, 8), y + 8] = pair[:, 4:8]
    k16 = lax.broadcasted_iota(jnp.int32, (16, 128), 0)
    l16 = lax.broadcasted_iota(jnp.int32, (16, 128), 1)
    pick_low = jnp.where((l16 == 128 - ZHALO + k16) & (k16 < ZHALO), 1.0, 0.0).astype(F32)
    pick_high = jnp.where((l16 == k16) & (k16 < ZHALO), 1.0, 0.0).astype(F32)
    for side, pick in enumerate((pick_low, pick_high)):
        for half in (0, 1):
            zsend[side, half] = lax.dot_general(
                pick, block[pl.ds(half * 4, 4)].reshape(128, 128), (((1,), (1,)), ((), ())),
                precision=lax.Precision.HIGHEST, preferred_element_type=F32,
            )
    pl.semaphore_wait(barrier, len(partners))

    span = {-1: (4, 12, 3), 0: (4, 4, 8), 1: (8, 0, 4)}
    sent = []
    copies = []
    for n, (dx, dy) in enumerate(XY8):
        (ax, bx, cx), (ay, by, cy) = span[dx], span[dy]
        copies.append(
            pltpu.make_async_remote_copy(
                src_ref=e0.at[pl.ds(ax, cx), pl.ds(ay, cy)],
                dst_ref=e0.at[pl.ds(bx, cx), pl.ds(by, cy)],
                send_sem=s0.at[n], recv_sem=q0.at[n],
                device_id=device(dx, dy, 0), device_id_type=MESH,
            )
        )
        copies[-1].start()
    n = 8
    for dz in (-1, 1):
        side = 0 if dz > 0 else 1
        for dx, dy in itertools.product((-1, 0, 1), repeat=2):
            first, count = {-1: (0, 1), 0: (0, 2), 1: (1, 1)}[dx]
            copies.append(
                pltpu.make_async_remote_copy(
                    src_ref=zsend.at[side, pl.ds(first, count)],
                    dst_ref=zrecv.at[side, 1 - dx, 1 - dy, pl.ds(first, count)],
                    send_sem=s0.at[n], recv_sem=q0.at[n],
                    device_id=device(dx, dy, dz), device_id_type=MESH,
                )
            )
            copies[-1].start()
            n += 1

    def rim2(x):
        m2[x] = jnp.zeros((28,) + TILE, F32)

    loop(0, 28, rim2)
    line = jnp.zeros((10,) + TILE, F32)
    for ref in (m2h, v2, vp2, u2h, up2, r2):
        ref[0] = line
    for ref in (v2, vp2, u2h, up2):
        ref[17] = line
    line = jnp.zeros((6,) + TILE, F32)
    m3[0] = line
    for ref in (v3, vp3, u3h, up3):
        ref[0] = line
        ref[9] = line

    def rim3(x):
        u3[x] = jnp.zeros((16,) + TILE, F32)

    loop(0, 16, rim3)
    for copy in copies:
        copy.wait_recv()
    sent += copies

    low_in, high_in = jnp.where(gz > 0, 1.0, 0.0), jnp.where(gz < SIDE - 1, 1.0, 0.0)
    put = jnp.concatenate([pick_low, pick_high], axis=0)
    for rx, ry in [(0, 0), (0, -1), (0, 1), (-1, 0), (1, 0), (-1, -1), (-1, 1), (1, -1), (1, 1)]:
        inside = None
        if rx:
            inside = gx > 0 if rx < 0 else gx < SIDE - 1
        if ry:
            more = gy > 0 if ry < 0 else gy < SIDE - 1
            inside = more if inside is None else inside & more
        factor = 1.0 if inside is None else jnp.where(inside, 1.0, 0.0)
        for half in {-1: (1,), 0: (0, 1), 1: (0,)}[rx]:
            both = jnp.concatenate([zrecv[0, rx + 1, ry + 1, half], zrecv[1, rx + 1, ry + 1, half]], axis=0)
            ends = lax.dot_general(
                both, put, (((0,), (0,)), ((), ())),
                precision=lax.Precision.HIGHEST, preferred_element_type=F32,
            ).reshape((4, 4) + TILE)
            x_at, nx = 4 + 8 * rx + 4 * half, 3 if rx > 0 else 4
            for late in {-1: (1,), 0: (0, 1), 1: (0,)}[ry]:
                y_at, ny = 4 + 8 * ry + 4 * late, 3 if ry > 0 else 4
                shape = (nx, ny) + TILE
                spot = (pl.ds(x_at, nx), pl.ds(y_at, ny))
                top, lane = rows(shape) < 4, lanes(shape)
                held = ends[0:nx, 0:ny]
                if not late:
                    held = turn_rows(held, 4)
                whole = jnp.where(top, twice(e0[spot]), held)
                dens = jnp.where(top, spread(whole, 3), spread(whole, 7))
                ok = jnp.where(
                    top, 1.0,
                    jnp.where(lane < ZHALO, high_in, jnp.where(lane >= 128 - ZHALO, low_in, 0.0)),
                ) * factor
                g0[spot] = (1.8 * ok) * whole
                m0[spot] = (0.15 * ok) * (0.001 + (1.0 - 0.001) * (dens * dens * dens))

    diagonal(m0, d0, i0, (1, 15), (1, 14), down_pair)
    first_sweep(i0, g0, v0, vp0, (1, 15), (1, 14), up_pair)
    smooth(v0, vp0, m0, i0, g0, u0, up0, (2, 14), (2, 12), up_pair, down_pair)
    residual(u0, up0, m0, d0, g0, r0, (3, 12), (3, 9), down_pair)
    restrict_xy(r0, t1, 4, 4, 4)
    coarsen_xy(m0, tm1, 4, 4, 4)
    top128 = rows((16,) + TILE) < 4

    def both_ends(tiles, kind):
        flat = tiles[...].reshape(128, 128)
        parts = [product(flat, kind(where)).reshape((16,) + TILE) for where in ("all", "beyond")]
        joined = jnp.where(top128, parts[0], parts[1])
        return joined + turn_rows(joined, 4)

    new_g, new_m = both_ends(t1, restriction), both_ends(tm1, coarsening)
    joined = jnp.where(rows((16,) + TILE) == 3, new_m, new_g)[:, 0:4]
    e1[pl.ds(4, 4), pl.ds(4, 4)] = joined.reshape(4, 4, 4, 128)

    def blocks8(ref, send, recv):
        found = []
        for n, (dx, dy) in enumerate(XY8):
            found.append(
                pltpu.make_async_remote_copy(
                    src_ref=ref.at[pl.ds(4, 4), pl.ds(4, 4)],
                    dst_ref=ref.at[pl.ds({-1: 8, 0: 4, 1: 0}[dx], 4), pl.ds({-1: 8, 0: 4, 1: 0}[dy], 4)],
                    send_sem=send.at[n], recv_sem=recv.at[n],
                    device_id=device(dx, dy, 0), device_id_type=MESH,
                )
            )
        return found

    copies = blocks8(e1, s1, q1)
    for copy in copies:
        copy.start()

    line = new_m.reshape((4, 4) + TILE)
    line = line[:, 0] + line[:, 1], line[:, 2] + line[:, 3]
    flat = jnp.stack([line[y][2 * x] + line[y][2 * x + 1] for x in (0, 1) for y in (0, 1)], axis=0)
    flat = product(flat.reshape(32, 128), coarsening("round")).reshape((4,) + TILE)
    line = flat[0]
    for k in (1, 2, 3):
        line = jnp.where(rows() == k, flat[k], line)
    yzm[1, gy] = jnp.where(lanes() < 32, line, 0.0)[0:4]
    m_copies = []
    for n, (dy, dz) in enumerate(YZ23):
        m_copies.append(
            pltpu.make_async_remote_copy(
                src_ref=yzm.at[1, gy],
                dst_ref=yzm.at[1 - dz, gy],
                send_sem=sym.at[n], recv_sem=qym.at[n],
                device_id=device(0, dy, dz), device_id_type=MESH,
            )
        )
    for copy in m_copies:
        copy.start()
    sent += m_copies
    for copy in copies:
        copy.wait_recv()
    sent += copies

    y_index = lax.broadcasted_iota(jnp.int32, (12,) + TILE, 0)
    inside_y = jnp.where(y_index < 4, jnp.where(gy > 0, 1.0, 0.0), jnp.where(y_index < 8, 1.0, jnp.where(gy < SIDE - 1, 1.0, 0.0)))

    def take1(x):
        inside_x = jnp.where(((x >= 4) | (gx > 0)) & ((x < 8) | (gx < SIDE - 1)), 1.0, 0.0)
        whole = twice(e1[x]) * (inside_x * inside_y)
        mod = spread(whole, 3)
        m1[x] = mod
        g1[x] = jnp.where(mod > 0.0, whole, 0.0)

    loop(0, 12, take1)
    diagonal(m1, d1, i1, (1, 12), (1, 11), down_plain)
    first_sweep(i1, g1, v1, vp1, (1, 12), (1, 11), up_plain)
    smooth(v1, vp1, m1, i1, g1, u1, up1, (2, 9), (2, 7), up_plain, down_plain)
    own = (pl.ds(4, 4), pl.ds(4, 4))
    u1x[own] = u1[own][:, :, 0:4]
    u_copies = blocks8(u1x, s1u, q1u)
    residual(u1, up1, m1, d1, g1, r1, (3, 8), (3, 5), down_plain)
    restrict_xy(r1, t2, 4, 2, 2)
    new_g = product(t2[...].reshape(32, 128), restriction("round"))
    both = new_g.reshape((4,) + TILE)
    group = lanes((4,) + TILE) // 32
    packed = jnp.where(group == 0, spread(both, 0), 0.0)
    for f in (1, 2):
        packed = jnp.where(group == f, spread(turn_lanes(both, 32 * f), f), packed)
    line = packed[0]
    for k in (1, 2, 3):
        line = jnp.where(rows() == k, packed[k], line)
    yz[1, gy] = line[0:4]

    copies = []
    for n, (dy, dz) in enumerate(YZ23):
        copies.append(
            pltpu.make_async_remote_copy(
                src_ref=yz.at[1, gy],
                dst_ref=yz.at[1 - dz, gy],
                send_sem=sy.at[n], recv_sem=qy.at[n],
                device_id=device(0, dy, dz), device_id_type=MESH,
            )
        )
    for copy in copies:
        copy.start()
    sent += copies

    for copy in m_copies:
        copy.wait_recv()
    xm[gx] = yzm[1] + turn_lanes(yzm[0], 96) * low_in + turn_lanes(yzm[2], 32) * high_in
    m_copies = []
    for n, dx in enumerate(RING):
        m_copies.append(
            pltpu.make_async_remote_copy(
                src_ref=xm.at[gx],
                dst_ref=xm.at[gx],
                send_sem=sxm.at[n], recv_sem=qxm.at[n],
                device_id=device(dx, 0, 0), device_id_type=MESH,
            )
        )
    for copy in m_copies:
        copy.start()
    sent += m_copies

    for copy in copies:
        copy.wait_recv()
    shape = (8,) + TILE
    group, field = lanes(shape) // 32, rows(shape) % 4
    is_own = group == field
    is_high, is_low = group == (field + 1) % 4, group == (field + 3) % 4
    low = twice(turn_lanes(yz[0], 96) * low_in)
    own = twice(yz[1])
    high = twice(turn_lanes(yz[2], 32) * high_in)
    columns = []
    for k in range(4):
        whole = jnp.where(is_high, spread(high, k), 0.0)
        whole = jnp.where(is_low, spread(low, k), whole)
        whole = jnp.where(is_own, spread(own, k), whole)
        second = turn_lanes(whole, 96)
        third = spread(turn_lanes(whole, 64), 2)
        here = lanes(shape)
        line = jnp.where((here >= 54) & (here < 107), turn_lanes(third, 75), whole)
        other = jnp.where((here >= 54) & (here < 76), turn_lanes(third, 22), second)
        columns.append(jnp.where(field == 0, line, other))
    for x in range(2):
        for y in range(8):
            x2[2 * gx + x, 2 * y] = columns[2 * x][y, 0:2]
            x2[2 * gx + x, 2 * y + 1] = columns[2 * x + 1][y, 0:2]

    copies = []
    for n, dx in enumerate(RING):
        copies.append(
            pltpu.make_async_remote_copy(
                src_ref=x2.at[pl.ds(2 * gx, 2)],
                dst_ref=x2.at[pl.ds(2 * gx, 2)],
                send_sem=sx.at[n], recv_sem=qx.at[n],
                device_id=device(dx, 0, 0), device_id_type=MESH,
            )
        )
    for copy in copies:
        copy.start()
    sent += copies

    for copy in m_copies:
        copy.wait_recv()

    def take_m(i):
        tile = twice(xm[i])
        for x in range(2):
            pair = jnp.stack([spread(tile, 2 * x), spread(tile, 2 * x + 1)], axis=1)
            mod = pair.reshape((16,) + TILE)
            m2[2 * i + x + 6, pl.ds(6, 16)] = mod
            mod = jnp.where(rows((8,) + TILE) < 4, mod[0:8], mod[8:16])
            m2h[2 * i + x + 1, pl.ds(1, 8)] = mod
            put_rims(m2h, 2 * i + x + 1, mod)

    loop(0, 8, take_m)

    def whole2(ref):
        def store(x, line):
            first, second = halves(line)
            ref[x + 5, pl.ds(6, 8)] = first
            ref[x + 5, pl.ds(14, 8)] = second

        return store

    diagonal(m2h, d2, i2h, (1, 17), (1, 8), down_plain, whole2(i2))
    coarsen_xy(m2h, tm3, 1, 8, 4)
    new_m = product(tm3[...].reshape(256, 128), coarsening("round")).reshape(8, 4, 8, 128)
    for x in range(8):
        m3[x + 1, pl.ds(1, 4)] = new_m[x]
        put_rims(m3, x + 1, new_m[x])
    diagonal(m3, d3, i3, (1, 9), (1, 4), down_plain)
    for copy in copies:
        copy.wait_recv()

    for copy in u_copies:
        copy.start()
    sent += u_copies

    def take2(x):
        whole = twice(twice(x2[x]))
        here = lanes(whole.shape)
        third = jnp.where(
            (here < 32) | (here >= 107),
            turn_lanes(spread(whole, 0), 128 - 75),
            turn_lanes(spread(whole, 1), 128 - 22),
        )
        whole = jnp.where(rows(whole.shape) % 4 == 2, third, whole)
        whole = jnp.where(m2[x + 6, pl.ds(6, 16)] > 0.0, whole, 0.0)
        g2[x + 6, pl.ds(6, 16)] = whole
        g2h[x + 1, pl.ds(1, 8)] = jnp.where(rows((8,) + TILE) < 4, whole[0:8], whole[8:16])

    loop(0, 16, take2)

    span = ((1, 17), (1, 8), up_plain, down_plain, True)
    first_sweep(i2h, g2h, v2, vp2, (1, 17), (1, 8), up_plain, True)
    smooth(v2, vp2, m2h, i2h, g2h, u2h, up2, *span, whole2(u2))
    residual(u2h, up2, m2h, d2, g2h, r2, (1, 17), (1, 8), down_plain, True)
    restrict_xy(r2, t3, 1, 8, 4)
    new_g = product(t3[...].reshape(256, 128), restriction("round")).reshape(8, 4, 8, 128)
    for x in range(8):
        g3[x + 1, pl.ds(1, 4)] = jnp.where(m3[x + 1, pl.ds(1, 4)] > 0.0, new_g[x], 0.0)

    span = ((1, 9), (1, 4), up_plain, down_plain, True)
    first_sweep(i3, g3, v3, vp3, (1, 9), (1, 4), up_plain, True)

    def two(i):
        smooth(v3, vp3, m3, i3, g3, u3h, up3, *span)
        smooth(u3h, up3, m3, i3, g3, v3, vp3, *span)

    loop_rolled(0, 3, two)

    def whole3(x, line):
        first, second = halves(line)
        u3[x + 3, pl.ds(4, 4)] = first
        u3[x + 3, pl.ds(8, 4)] = second

    smooth(v3, vp3, m3, i3, g3, u3h, up3, *span, whole3)

    x_at, y_at = 2 * gx + 2, 2 * gy + 2
    rise(
        u3[pl.ds(gx + 2, 7), pl.ds(gy + 2, 7)],
        (prolongation("round"),),
        lambda x: u2[x + x_at, pl.ds(y_at, 12)],
        (m2, x_at, y_at), (i2, x_at, y_at), (g2, x_at, y_at),
        zs, c, cp, a, ap, f2, up_plain, down_plain,
    )
    for copy in u_copies:
        copy.wait_recv()
    rise(
        f2[pl.ds(0, 7), pl.ds(0, 7)],
        (prolongation("round"),),
        lambda x: twice(u1x[x]),
        (m1, 0, 0), (i1, 0, 0), (g1, 0, 0),
        zs, c, cp, a, ap, f1, up_plain, down_plain,
    )

    rise(
        f1[pl.ds(1, 7), pl.ds(1, 7)],
        (prolongation("all"), prolongation("beyond")),
        lambda x: u0[x + 2, pl.ds(2, 12)],
        (m0, 2, 2), (i0, 2, 2), (g0, 2, 2),
        zs, c, cp, a, ap, f0, up_pair, down_pair,
    )
    for f in range(3):
        plane = f0[:, f]
        for y in range(8):
            if y != f:
                plane = jnp.where(rows((8,) + TILE) == y, turn_rows(f0[:, y], (y - f) % 8), plane)
        out[f] = plane
    for copy in sent:
        copy.wait_send()


def per_device(loads, density):
    def tiles(*lead):
        return pltpu.VMEM(lead + TILE, F32)

    def thin(*lead):
        return pltpu.VMEM(lead + (4, 128), F32)

    sems = [pltpu.SemaphoreType.DMA((2,))]
    for count in (26, 8, 8, 23, 7, 23, 7):
        sems += [pltpu.SemaphoreType.DMA((count,))] * 2
    return pl.pallas_call(
        kernel,
        out_shape=jax.ShapeDtypeStruct((3,) + (8,) + TILE, F32),
        in_specs=[pl.BlockSpec(memory_space=pl.ANY)] * 2,
        out_specs=pl.BlockSpec(memory_space=pltpu.VMEM),
        scratch_shapes=[tiles(3, 8), tiles(8), tiles(8, 4), thin(15, 15), pltpu.VMEM((2, 2, 16, 128), F32), pltpu.VMEM((2, 3, 3, 2, 16, 128), F32)]
        + [tiles(15, 15)] * 9
        + [tiles(4, 4)] * 2
        + [thin(12, 12)] * 2
        + [tiles(12, 12)] * 9
        + [tiles(2, 2)]
        + [thin(3, 8), thin(3, 8), thin(8, 8), pltpu.VMEM((16, 16, 2, 128), F32)]
        + [tiles(28, 28)] * 4
        + [tiles(18, 10)] * 9
        + [tiles(8, 4)] * 2
        + [tiles(16, 16)]
        + [tiles(10, 6)] * 8
        + [tiles(7, 7)]
        + [tiles(12, 12)] * 4
        + [tiles(8, 8)] * 3
        + sems,
        compiler_params=pltpu.CompilerParams(
            collective_id=0, has_side_effects=True, vmem_limit_bytes=60 * 2**20
        ),
        cost_estimate=pl.CostEstimate(flops=10**8, bytes_accessed=10**6, transcendentals=0),
    )(loads, density)


def solution(mesh):
    placed = (P(None, "gx", "gy", "gz"), P("gx", "gy", "gz"))
    return jax.shard_map(
        per_device, mesh=mesh, in_specs=placed, out_specs=P(None, "gx", "gy", "gz"), check_vma=False
    )
```

```python
import functools
import itertools

import jax
import jax.numpy as jnp
from jax import lax
from jax.experimental import pallas as pl
from jax.experimental.pallas import tpu as pltpu
from jax.sharding import PartitionSpec as P

MESH = pl.DeviceIdType.MESH
F32 = jnp.float32
TILE = (8, 128)
SIDE = 8
UNROLL = 16
ZHALO = 12
RING = (4, 3, -3, 2, -2, 1, -1)
XY8 = [(dx, dy) for dx in (-1, 0, 1) for dy in (-1, 0, 1) if dx or dy]
YZ23 = [(dy, dz) for dy in RING + (0,) for dz in (-1, 1, 0) if dy or dz]


def around():
    here = [lax.axis_index(axis) for axis in ("gx", "gy", "gz")]
    known = [{0: at} for at in here]

    def device(*steps):
        for at, seen, step in zip(here, known, steps):
            if step % SIDE not in seen:
                seen[step % SIDE] = lax.rem(at + step % SIDE, SIDE)
        return tuple(seen[step % SIDE] for seen, step in zip(known, steps))

    return device


def lanes(shape=TILE):
    return lax.broadcasted_iota(jnp.int32, shape, len(shape) - 1)


def rows(shape=TILE):
    return lax.broadcasted_iota(jnp.int32, shape, len(shape) - 2)


def turn_rows(tiles, by):
    return pltpu.roll(tiles, by, tiles.ndim - 2)


def turn_lanes(tiles, by):
    return pltpu.roll(tiles, by, tiles.ndim - 1)


def up_plain(tiles):
    return turn_lanes(tiles, 127)


def down_plain(tiles):
    return turn_lanes(tiles, 1)


def up_pair(tiles):
    turned = turn_lanes(tiles, 127)
    return jnp.where(lanes(tiles.shape) == 127, turn_rows(turned, 4), turned)


def down_pair(tiles):
    turned = turn_lanes(tiles, 1)
    return jnp.where(lanes(tiles.shape) == 0, turn_rows(turned, 4), turned)


def twice(tiles):
    return jnp.concatenate([tiles, tiles], axis=tiles.ndim - 2)


def spread(tiles, row):
    return jnp.broadcast_to(tiles[..., row : row + 1, :], tiles.shape)


def halves(tiles):
    top, turned = rows(tiles.shape) < 4, turn_rows(tiles, 4)
    return jnp.where(top, tiles, turned), jnp.where(top, turned, tiles)


def put_rims(ref, x, line):
    top, n = rows() < 4, line.shape[0]
    ref[x, 0] = jnp.where(top, 0.0, turn_rows(line[n - 1], 4))
    ref[x, n + 1] = jnp.where(top, turn_rows(line[0], 4), 0.0)


def stencil(v, vp, m, ix, y0, n, mx, my, down):
    wide = pl.ds(y0 - 1, n + 2)
    lower = {sx: v[ix + sx, wide] for sx in (-1, 0, 1)}
    upper = {sx: vp[ix + sx, wide] for sx in (-1, 0, 1)}
    weights = {-1: m[mx - 1, pl.ds(y0 + my - 1, n + 1)], 1: m[mx, pl.ds(y0 + my - 1, n + 1)]}
    above, below = None, None
    for sx in (-1, 1):
        both = lower[sx] + upper[sx]
        for sy in (-1, 1):
            side = slice(1 + sy, 1 + sy + n)
            weight = weights[sx][0:n] if sy < 0 else weights[sx][1 : n + 1]
            hi = weight * (both[side] + (upper[sx][1 : n + 1] + upper[0][side]))
            lo = weight * (both[side] + (lower[sx][1 : n + 1] + lower[0][side]))
            above = hi if above is None else above + hi
            below = lo if below is None else below + lo
    return above + down(below)


def loop(lower, upper, body):
    count = upper - lower
    each = max(k for k in range(1, UNROLL + 1) if count % k == 0)

    def step(i, carry):
        for k in range(each):
            body(lower + i * each + k)
        return carry

    if each == count:
        step(0, 0)
    else:
        lax.fori_loop(0, count // each, step, 0)


def loop_rolled(lower, upper, body):
    def step(i, carry):
        body(i)
        return carry

    lax.fori_loop(lower, upper, step, 0)


def diagonal(m, d4, inv, xs, ys, down, also=None):
    y0, n = ys
    at = pl.ds(y0, n)

    def body(x):
        pairs = m[x - 1, pl.ds(y0 - 1, n + 1)] + m[x, pl.ds(y0 - 1, n + 1)]
        four = pairs[0:n] + pairs[1 : n + 1]
        total = four + down(four)
        share = jnp.where(m[x, at] > 0.0, 0.15 / total, 0.0)
        d4[x, at] = 4.0 * total
        inv[x, at] = share
        if also is not None:
            also(x, share)

    loop(xs[0], xs[1], body)


def first_sweep(inv, g, v, vp, xs, ys, up, rims=False):
    y0, n = ys
    at = pl.ds(y0, n)

    def body(x):
        first = inv[x, at] * g[x, at]
        above = up(first)
        v[x, at] = first
        vp[x, at] = above
        if rims:
            put_rims(v, x, first)
            put_rims(vp, x, above)

    loop(xs[0], xs[1], body)


def smooth(v, vp, m, inv, g, out, outp, xs, ys, up, down, rims=False, also=None):
    y0, n = ys
    at = pl.ds(y0, n)

    def body(x):
        around = stencil(v, vp, m, x, y0, n, x, 0, down)
        new = 0.4 * v[x, at] + inv[x, at] * (g[x, at] + around)
        above = up(new)
        out[x, at] = new
        outp[x, at] = above
        if rims:
            put_rims(out, x, new)
            put_rims(outp, x, above)
        if also is not None:
            also(x, new)

    loop(xs[0], xs[1], body)


def residual(v, vp, m, d4, g, out, xs, ys, down, rims=False):
    y0, n = ys
    at = pl.ds(y0, n)

    def body(x):
        around = stencil(v, vp, m, x, y0, n, x, 0, down)
        left = (g[x, at] - d4[x, at] * v[x, at]) + around
        out[x, at] = left
        if rims:
            put_rims(out, x, left)

    loop(xs[0], xs[1], body)


def restrict_xy(res, out, base, count_x, count):
    def body(i):
        x = base + 2 * i
        wide = pl.ds(base - 1, 2 * count + 1)
        line = res[x, wide] + 0.5 * (res[x - 1, wide] + res[x + 1, wide])
        for k in range(count):
            out[i, k] = line[2 * k + 1] + 0.5 * (line[2 * k] + line[2 * k + 2])

    loop(0, count_x, body)


def coarsen_xy(m, out, base, count_x, count):
    def body(i):
        x = base + 2 * i
        wide = pl.ds(base, 2 * count)
        line = m[x, wide] + m[x + 1, wide]
        for k in range(count):
            out[i, k] = line[2 * k] + line[2 * k + 1]

    loop(0, count_x, body)


def place(index, own):
    if own == "all":
        return index
    if own == "beyond":
        return jnp.where(index < 64, index + 128, index - 128)
    return jnp.where(index < 96, index, index - 128)


def restriction(fine):
    f = place(lax.broadcasted_iota(jnp.int32, (128, 128), 0), fine)
    c = place(lax.broadcasted_iota(jnp.int32, (128, 128), 1), "round")
    gap = f - 2 * c
    return jnp.where(gap == 0, 0.5, jnp.where((gap == 1) | (gap == -1), 0.25, 0.0)).astype(F32)


def coarsening(fine):
    f = place(lax.broadcasted_iota(jnp.int32, (128, 128), 0), fine)
    c = place(lax.broadcasted_iota(jnp.int32, (128, 128), 1), "round")
    gap = f - 2 * c
    return jnp.where((gap == 0) | (gap == 1), 0.125, 0.0).astype(F32)


def prolongation(fine):
    c = place(lax.broadcasted_iota(jnp.int32, (128, 128), 0), "round")
    f = place(lax.broadcasted_iota(jnp.int32, (128, 128), 1), fine)
    gap = f - 2 * c
    return jnp.where(gap == 0, 1.0, jnp.where((gap == 1) | (gap == -1), 0.5, 0.0)).astype(F32)


def product(a, b):
    return jnp.dot(a, b, precision=lax.Precision.HIGHEST, preferred_element_type=F32)


def rise(source, mats, before, m, inv, g, zs, c, cp, a, ap, out, up, down):
    flat = source.reshape(7 * 7 * 8, 128)
    wide = product(flat, mats[0])
    if len(mats) == 2:
        top = lax.broadcasted_iota(jnp.int32, (7 * 7 * 8, 128), 0) % 8 < 4
        wide = jnp.where(top, wide, product(flat, mats[1]))
    zs[...] = wide.reshape(7, 7, 8, 128)
    m_ref, mx, my = m
    i_ref, ix, iy = inv
    g_ref, gx, gy = g

    def correct(i):
        for half in (0, 1):
            x = 2 * i + half
            line = zs[i] if half == 0 else 0.5 * (zs[i] + zs[i + 1])
            middle = 0.5 * (line[0:6] + line[1:7])
            add = jnp.stack([line[0:6], middle], axis=1).reshape((12,) + TILE)
            new = jnp.where(m_ref[x + mx, pl.ds(my, 12)] > 0.0, before(x) + add, 0.0)
            c[x] = new
            cp[x] = up(new)

    loop(0, 6, correct)

    def sweep(old, oldp, x, y0, n):
        around = stencil(old, oldp, m_ref, x, y0, n, x + mx, my, down)
        new = 0.4 * old[x, pl.ds(y0, n)] + i_ref[x + ix, pl.ds(y0 + iy, n)] * (
            g_ref[x + gx, pl.ds(y0 + gy, n)] + around
        )
        return jnp.where(m_ref[x + mx, pl.ds(y0 + my, n)] > 0.0, new, 0.0)

    def sweep_a(x):
        new = sweep(c, cp, x, 1, 10)
        a[x, pl.ds(1, 10)] = new
        ap[x, pl.ds(1, 10)] = up(new)

    loop(1, 11, sweep_a)

    def sweep_b(x):
        out[x - 2] = sweep(a, ap, x, 2, 8)

    loop(2, 10, sweep_b)


def kernel(
    loads, density, out, held_loads, held_density, block, e0, zsend, zrecv, g0, m0, d0, i0, v0, vp0, u0, up0, r0,
    t1, tm1, e1, u1x, g1, m1, d1, i1, v1, vp1, u1, up1, r1,
    t2, yz, yzm, xm, x2, g2, m2, i2, u2, g2h, m2h, d2, i2h, v2, vp2, u2h, up2, r2,
    t3, tm3, u3, g3, m3, d3, i3, v3, vp3, u3h, up3,
    zs, c, cp, a, ap, f2, f1, f0,
    sin, s0, q0, s1, q1, s1u, q1u, sy, qy, sx, qx, sym, qym, sxm, qxm,
):
    device = around()
    gx, gy, gz = device(0, 0, 0)

    inputs = [
        pltpu.make_async_copy(loads, held_loads, sin.at[0]),
        pltpu.make_async_copy(density, held_density, sin.at[1]),
    ]
    for copy in inputs:
        copy.start()
    for step in RING:
        device(step, step, step)

    partners = {(dx, dy, dz) for dx in (-1, 0, 1) for dy in (-1, 0, 1) for dz in (-1, 0, 1)}
    partners |= {(0, dy, dz) for dy, dz in YZ23} | {(dx, 0, 0) for dx in RING}
    partners = sorted(partners - {(0, 0, 0)})
    barrier = pltpu.get_barrier_semaphore()
    for o in partners:
        pl.semaphore_signal(barrier, inc=1, device_id=device(*o), device_id_type=MESH)

    for copy in inputs:
        copy.wait()
    field = rows((8,) + TILE) % 4
    four = [held_loads[0], held_loads[1], held_loads[2], held_density[...]]
    for y in range(4):
        pair = turn_rows(four[3], (3 - y) % 8) if y != 3 else four[3]
        for f in range(3):
            pair = jnp.where(field == f, turn_rows(four[f], (f - y) % 8) if f != y else four[f], pair)
        block[:, y] = pair
        e0[pl.ds(4, 8), y + 4] = pair[:, 0:4]
        e0[pl.ds(4, 8), y + 8] = pair[:, 4:8]
    k16 = lax.broadcasted_iota(jnp.int32, (16, 128), 0)
    l16 = lax.broadcasted_iota(jnp.int32, (16, 128), 1)
    pick_low = jnp.where((l16 == 128 - ZHALO + k16) & (k16 < ZHALO), 1.0, 0.0).astype(F32)
    pick_high = jnp.where((l16 == k16) & (k16 < ZHALO), 1.0, 0.0).astype(F32)
    for side, pick in enumerate((pick_low, pick_high)):
        for half in (0, 1):
            zsend[side, half] = lax.dot_general(
                pick, block[pl.ds(half * 4, 4)].reshape(128, 128), (((1,), (1,)), ((), ())),
                precision=lax.Precision.HIGHEST, preferred_element_type=F32,
            )
    pl.semaphore_wait(barrier, len(partners))

    span = {-1: (4, 12, 3), 0: (4, 4, 8), 1: (8, 0, 4)}
    sent = []
    copies = []
    for n, (dx, dy) in enumerate(XY8):
        (ax, bx, cx), (ay, by, cy) = span[dx], span[dy]
        copies.append(
            pltpu.make_async_remote_copy(
                src_ref=e0.at[pl.ds(ax, cx), pl.ds(ay, cy)],
                dst_ref=e0.at[pl.ds(bx, cx), pl.ds(by, cy)],
                send_sem=s0.at[n], recv_sem=q0.at[n],
                device_id=device(dx, dy, 0), device_id_type=MESH,
            )
        )
        copies[-1].start()
    n = 8
    for dz in (-1, 1):
        side = 0 if dz > 0 else 1
        for dx, dy in itertools.product((-1, 0, 1), repeat=2):
            first, count = {-1: (0, 1), 0: (0, 2), 1: (1, 1)}[dx]
            copies.append(
                pltpu.make_async_remote_copy(
                    src_ref=zsend.at[side, pl.ds(first, count)],
                    dst_ref=zrecv.at[side, 1 - dx, 1 - dy, pl.ds(first, count)],
                    send_sem=s0.at[n], recv_sem=q0.at[n],
                    device_id=device(dx, dy, dz), device_id_type=MESH,
                )
            )
            copies[-1].start()
            n += 1

    def rim2(x):
        m2[x] = jnp.zeros((28,) + TILE, F32)

    loop(0, 28, rim2)
    line = jnp.zeros((10,) + TILE, F32)
    for ref in (m2h, v2, vp2, u2h, up2, r2):
        ref[0] = line
    for ref in (v2, vp2, u2h, up2):
        ref[17] = line
    line = jnp.zeros((6,) + TILE, F32)
    m3[0] = line
    for ref in (v3, vp3, u3h, up3):
        ref[0] = line
        ref[9] = line

    def rim3(x):
        u3[x] = jnp.zeros((16,) + TILE, F32)

    loop(0, 16, rim3)
    for copy in copies:
        copy.wait_recv()
    sent += copies

    low_in, high_in = jnp.where(gz > 0, 1.0, 0.0), jnp.where(gz < SIDE - 1, 1.0, 0.0)
    put = jnp.concatenate([pick_low, pick_high], axis=0)
    for rx, ry in [(0, 0), (0, -1), (0, 1), (-1, 0), (1, 0), (-1, -1), (-1, 1), (1, -1), (1, 1)]:
        inside = None
        if rx:
            inside = gx > 0 if rx < 0 else gx < SIDE - 1
        if ry:
            more = gy > 0 if ry < 0 else gy < SIDE - 1
            inside = more if inside is None else inside & more
        factor = 1.0 if inside is None else jnp.where(inside, 1.0, 0.0)
        for half in {-1: (1,), 0: (0, 1), 1: (0,)}[rx]:
            both = jnp.concatenate([zrecv[0, rx + 1, ry + 1, half], zrecv[1, rx + 1, ry + 1, half]], axis=0)
            ends = lax.dot_general(
                both, put, (((0,), (0,)), ((), ())),
                precision=lax.Precision.HIGHEST, preferred_element_type=F32,
            ).reshape((4, 4) + TILE)
            x_at, nx = 4 + 8 * rx + 4 * half, 3 if rx > 0 else 4
            for late in {-1: (1,), 0: (0, 1), 1: (0,)}[ry]:
                y_at, ny = 4 + 8 * ry + 4 * late, 3 if ry > 0 else 4
                shape = (nx, ny) + TILE
                spot = (pl.ds(x_at, nx), pl.ds(y_at, ny))
                top, lane = rows(shape) < 4, lanes(shape)
                held = ends[0:nx, 0:ny]
                if not late:
                    held = turn_rows(held, 4)
                whole = jnp.where(top, twice(e0[spot]), held)
                dens = jnp.where(top, spread(whole, 3), spread(whole, 7))
                ok = jnp.where(
                    top, 1.0,
                    jnp.where(lane < ZHALO, high_in, jnp.where(lane >= 128 - ZHALO, low_in, 0.0)),
                ) * factor
                g0[spot] = (1.8 * ok) * whole
                m0[spot] = (0.15 * ok) * (0.001 + (1.0 - 0.001) * (dens * dens * dens))

    diagonal(m0, d0, i0, (1, 15), (1, 14), down_pair)
    first_sweep(i0, g0, v0, vp0, (1, 15), (1, 14), up_pair)
    smooth(v0, vp0, m0, i0, g0, u0, up0, (2, 14), (2, 12), up_pair, down_pair)
    residual(u0, up0, m0, d0, g0, r0, (3, 12), (3, 9), down_pair)
    restrict_xy(r0, t1, 4, 4, 4)
    coarsen_xy(m0, tm1, 4, 4, 4)
    top128 = rows((16,) + TILE) < 4

    def both_ends(tiles, kind):
        flat = tiles[...].reshape(128, 128)
        parts = [product(flat, kind(where)).reshape((16,) + TILE) for where in ("all", "beyond")]
        joined = jnp.where(top128, parts[0], parts[1])
        return joined + turn_rows(joined, 4)

    new_g, new_m = both_ends(t1, restriction), both_ends(tm1, coarsening)
    joined = jnp.where(rows((16,) + TILE) == 3, new_m, new_g)[:, 0:4]
    e1[pl.ds(4, 4), pl.ds(4, 4)] = joined.reshape(4, 4, 4, 128)

    def blocks8(ref, send, recv):
        found = []
        for n, (dx, dy) in enumerate(XY8):
            found.append(
                pltpu.make_async_remote_copy(
                    src_ref=ref.at[pl.ds(4, 4), pl.ds(4, 4)],
                    dst_ref=ref.at[pl.ds({-1: 8, 0: 4, 1: 0}[dx], 4), pl.ds({-1: 8, 0: 4, 1: 0}[dy], 4)],
                    send_sem=send.at[n], recv_sem=recv.at[n],
                    device_id=device(dx, dy, 0), device_id_type=MESH,
                )
            )
        return found

    copies = blocks8(e1, s1, q1)
    for copy in copies:
        copy.start()

    line = new_m.reshape((4, 4) + TILE)
    line = line[:, 0] + line[:, 1], line[:, 2] + line[:, 3]
    flat = jnp.stack([line[y][2 * x] + line[y][2 * x + 1] for x in (0, 1) for y in (0, 1)], axis=0)
    flat = product(flat.reshape(32, 128), coarsening("round")).reshape((4,) + TILE)
    line = flat[0]
    for k in (1, 2, 3):
        line = jnp.where(rows() == k, flat[k], line)
    yzm[1, gy] = jnp.where(lanes() < 32, line, 0.0)[0:4]
    m_copies = []
    for n, (dy, dz) in enumerate(YZ23):
        m_copies.append(
            pltpu.make_async_remote_copy(
                src_ref=yzm.at[1, gy],
                dst_ref=yzm.at[1 - dz, gy],
                send_sem=sym.at[n], recv_sem=qym.at[n],
                device_id=device(0, dy, dz), device_id_type=MESH,
            )
        )
    for copy in m_copies:
        copy.start()
    sent += m_copies
    for copy in copies:
        copy.wait_recv()
    sent += copies

    y_index = lax.broadcasted_iota(jnp.int32, (12,) + TILE, 0)
    inside_y = jnp.where(y_index < 4, jnp.where(gy > 0, 1.0, 0.0), jnp.where(y_index < 8, 1.0, jnp.where(gy < SIDE - 1, 1.0, 0.0)))

    def take1(x):
        inside_x = jnp.where(((x >= 4) | (gx > 0)) & ((x < 8) | (gx < SIDE - 1)), 1.0, 0.0)
        whole = twice(e1[x]) * (inside_x * inside_y)
        mod = spread(whole, 3)
        m1[x] = mod
        g1[x] = jnp.where(mod > 0.0, whole, 0.0)

    loop(0, 12, take1)
    diagonal(m1, d1, i1, (1, 12), (1, 11), down_plain)
    first_sweep(i1, g1, v1, vp1, (1, 12), (1, 11), up_plain)
    smooth(v1, vp1, m1, i1, g1, u1, up1, (2, 9), (2, 7), up_plain, down_plain)
    own = (pl.ds(4, 4), pl.ds(4, 4))
    u1x[own] = u1[own][:, :, 0:4]
    u_copies = blocks8(u1x, s1u, q1u)
    residual(u1, up1, m1, d1, g1, r1, (3, 8), (3, 5), down_plain)
    restrict_xy(r1, t2, 4, 2, 2)
    new_g = product(t2[...].reshape(32, 128), restriction("round"))
    both = new_g.reshape((4,) + TILE)
    group = lanes((4,) + TILE) // 32
    packed = jnp.where(group == 0, spread(both, 0), 0.0)
    for f in (1, 2):
        packed = jnp.where(group == f, spread(turn_lanes(both, 32 * f), f), packed)
    line = packed[0]
    for k in (1, 2, 3):
        line = jnp.where(rows() == k, packed[k], line)
    yz[1, gy] = line[0:4]

    copies = []
    for n, (dy, dz) in enumerate(YZ23):
        copies.append(
            pltpu.make_async_remote_copy(
                src_ref=yz.at[1, gy],
                dst_ref=yz.at[1 - dz, gy],
                send_sem=sy.at[n], recv_sem=qy.at[n],
                device_id=device(0, dy, dz), device_id_type=MESH,
            )
        )
    for copy in copies:
        copy.start()
    sent += copies

    for copy in m_copies:
        copy.wait_recv()
    xm[gx] = yzm[1] + turn_lanes(yzm[0], 96) * low_in + turn_lanes(yzm[2], 32) * high_in
    m_copies = []
    for n, dx in enumerate(RING):
        m_copies.append(
            pltpu.make_async_remote_copy(
                src_ref=xm.at[gx],
                dst_ref=xm.at[gx],
                send_sem=sxm.at[n], recv_sem=qxm.at[n],
                device_id=device(dx, 0, 0), device_id_type=MESH,
            )
        )
    for copy in m_copies:
        copy.start()
    sent += m_copies

    for copy in copies:
        copy.wait_recv()
    shape = (8,) + TILE
    group, field = lanes(shape) // 32, rows(shape) % 4
    is_own = group == field
    is_high, is_low = group == (field + 1) % 4, group == (field + 3) % 4
    low = twice(turn_lanes(yz[0], 96) * low_in)
    own = twice(yz[1])
    high = twice(turn_lanes(yz[2], 32) * high_in)
    columns = []
    for k in range(4):
        whole = jnp.where(is_high, spread(high, k), 0.0)
        whole = jnp.where(is_low, spread(low, k), whole)
        whole = jnp.where(is_own, spread(own, k), whole)
        second = turn_lanes(whole, 96)
        third = spread(turn_lanes(whole, 64), 2)
        here = lanes(shape)
        line = jnp.where((here >= 54) & (here < 107), turn_lanes(third, 75), whole)
        other = jnp.where((here >= 54) & (here < 76), turn_lanes(third, 22), second)
        columns.append(jnp.where(field == 0, line, other))
    for x in range(2):
        for y in range(8):
            x2[2 * gx + x, 2 * y] = columns[2 * x][y, 0:2]
            x2[2 * gx + x, 2 * y + 1] = columns[2 * x + 1][y, 0:2]

    copies = []
    for n, dx in enumerate(RING):
        copies.append(
            pltpu.make_async_remote_copy(
                src_ref=x2.at[pl.ds(2 * gx, 2)],
                dst_ref=x2.at[pl.ds(2 * gx, 2)],
                send_sem=sx.at[n], recv_sem=qx.at[n],
                device_id=device(dx, 0, 0), device_id_type=MESH,
            )
        )
    for copy in copies:
        copy.start()
    sent += copies

    for copy in m_copies:
        copy.wait_recv()

    def take_m(i):
        tile = twice(xm[i])
        for x in range(2):
            pair = jnp.stack([spread(tile, 2 * x), spread(tile, 2 * x + 1)], axis=1)
            mod = pair.reshape((16,) + TILE)
            m2[2 * i + x + 6, pl.ds(6, 16)] = mod
            mod = jnp.where(rows((8,) + TILE) < 4, mod[0:8], mod[8:16])
            m2h[2 * i + x + 1, pl.ds(1, 8)] = mod
            put_rims(m2h, 2 * i + x + 1, mod)

    loop(0, 8, take_m)

    def whole2(ref):
        def store(x, line):
            first, second = halves(line)
            ref[x + 5, pl.ds(6, 8)] = first
            ref[x + 5, pl.ds(14, 8)] = second

        return store

    diagonal(m2h, d2, i2h, (1, 17), (1, 8), down_plain, whole2(i2))
    coarsen_xy(m2h, tm3, 1, 8, 4)
    new_m = product(tm3[...].reshape(256, 128), coarsening("round")).reshape(8, 4, 8, 128)
    for x in range(8):
        m3[x + 1, pl.ds(1, 4)] = new_m[x]
        put_rims(m3, x + 1, new_m[x])
    diagonal(m3, d3, i3, (1, 9), (1, 4), down_plain)
    for copy in copies:
        copy.wait_recv()

    for copy in u_copies:
        copy.start()
    sent += u_copies

    def take2(x):
        whole = twice(twice(x2[x]))
        here = lanes(whole.shape)
        third = jnp.where(
            (here < 32) | (here >= 107),
            turn_lanes(spread(whole, 0), 128 - 75),
            turn_lanes(spread(whole, 1), 128 - 22),
        )
        whole = jnp.where(rows(whole.shape) % 4 == 2, third, whole)
        whole = jnp.where(m2[x + 6, pl.ds(6, 16)] > 0.0, whole, 0.0)
        g2[x + 6, pl.ds(6, 16)] = whole
        g2h[x + 1, pl.ds(1, 8)] = jnp.where(rows((8,) + TILE) < 4, whole[0:8], whole[8:16])

    loop(0, 16, take2)

    span = ((1, 17), (1, 8), up_plain, down_plain, True)
    first_sweep(i2h, g2h, v2, vp2, (1, 17), (1, 8), up_plain, True)
    smooth(v2, vp2, m2h, i2h, g2h, u2h, up2, *span, whole2(u2))
    residual(u2h, up2, m2h, d2, g2h, r2, (1, 17), (1, 8), down_plain, True)
    restrict_xy(r2, t3, 1, 8, 4)
    new_g = product(t3[...].reshape(256, 128), restriction("round")).reshape(8, 4, 8, 128)
    for x in range(8):
        g3[x + 1, pl.ds(1, 4)] = jnp.where(m3[x + 1, pl.ds(1, 4)] > 0.0, new_g[x], 0.0)

    span = ((1, 9), (1, 4), up_plain, down_plain, True)
    first_sweep(i3, g3, v3, vp3, (1, 9), (1, 4), up_plain, True)

    def two(i):
        smooth(v3, vp3, m3, i3, g3, u3h, up3, *span)
        smooth(u3h, up3, m3, i3, g3, v3, vp3, *span)

    loop_rolled(0, 3, two)

    def whole3(x, line):
        first, second = halves(line)
        u3[x + 3, pl.ds(4, 4)] = first
        u3[x + 3, pl.ds(8, 4)] = second

    smooth(v3, vp3, m3, i3, g3, u3h, up3, *span, whole3)

    x_at, y_at = 2 * gx + 2, 2 * gy + 2
    rise(
        u3[pl.ds(gx + 2, 7), pl.ds(gy + 2, 7)],
        (prolongation("round"),),
        lambda x: u2[x + x_at, pl.ds(y_at, 12)],
        (m2, x_at, y_at), (i2, x_at, y_at), (g2, x_at, y_at),
        zs, c, cp, a, ap, f2, up_plain, down_plain,
    )
    for copy in u_copies:
        copy.wait_recv()
    rise(
        f2[pl.ds(0, 7), pl.ds(0, 7)],
        (prolongation("round"),),
        lambda x: twice(u1x[x]),
        (m1, 0, 0), (i1, 0, 0), (g1, 0, 0),
        zs, c, cp, a, ap, f1, up_plain, down_plain,
    )

    rise(
        f1[pl.ds(1, 7), pl.ds(1, 7)],
        (prolongation("all"), prolongation("beyond")),
        lambda x: u0[x + 2, pl.ds(2, 12)],
        (m0, 2, 2), (i0, 2, 2), (g0, 2, 2),
        zs, c, cp, a, ap, f0, up_pair, down_pair,
    )
    for f in range(3):
        plane = f0[:, f]
        for y in range(8):
            if y != f:
                plane = jnp.where(rows((8,) + TILE) == y, turn_rows(f0[:, y], (y - f) % 8), plane)
        out[f] = plane
    for copy in sent:
        copy.wait_send()


def per_device(loads, density):
    def tiles(*lead):
        return pltpu.VMEM(lead + TILE, F32)

    def thin(*lead):
        return pltpu.VMEM(lead + (4, 128), F32)

    sems = [pltpu.SemaphoreType.DMA((2,))]
    for count in (26, 8, 8, 23, 7, 23, 7):
        sems += [pltpu.SemaphoreType.DMA((count,))] * 2
    return pl.pallas_call(
        kernel,
        out_shape=jax.ShapeDtypeStruct((3,) + (8,) + TILE, F32),
        in_specs=[pl.BlockSpec(memory_space=pl.ANY)] * 2,
        out_specs=pl.BlockSpec(memory_space=pltpu.VMEM),
        scratch_shapes=[tiles(3, 8), tiles(8), tiles(8, 4), thin(15, 15), pltpu.VMEM((2, 2, 16, 128), F32), pltpu.VMEM((2, 3, 3, 2, 16, 128), F32)]
        + [tiles(15, 15)] * 9
        + [tiles(4, 4)] * 2
        + [thin(12, 12)] * 2
        + [tiles(12, 12)] * 9
        + [tiles(2, 2)]
        + [thin(3, 8), thin(3, 8), thin(8, 8), pltpu.VMEM((16, 16, 2, 128), F32)]
        + [tiles(28, 28)] * 4
        + [tiles(18, 10)] * 9
        + [tiles(8, 4)] * 2
        + [tiles(16, 16)]
        + [tiles(10, 6)] * 8
        + [tiles(7, 7)]
        + [tiles(12, 12)] * 4
        + [tiles(8, 8)] * 3
        + sems,
        compiler_params=pltpu.CompilerParams(
            collective_id=0, has_side_effects=True, vmem_limit_bytes=60 * 2**20
        ),
        cost_estimate=pl.CostEstimate(flops=10**8, bytes_accessed=10**6, transcendentals=0),
    )(loads, density)


def solution(mesh):
    placed = (P(None, "gx", "gy", "gz"), P("gx", "gy", "gz"))
    return jax.shard_map(
        per_device, mesh=mesh, in_specs=placed, out_specs=P(None, "gx", "gy", "gz"), check_vma=False
    )
```
